32 devices in a mesh: groups: 2 (over y), pix: 8 (over z, x), mem: 2 (over core).
Axes of the slice: x: 2, y: 2, z: 4, core: 2. Of those that a mesh axis runs over, the one named last changes fastest.
Arguments:
- features: bfloat16 [2, 8192, 256], P('mem', ('groups', 'pix')), parts along dimension 1, may hold values from -6 to 6
- neighbours: int32 [9, 4096], P(None, 'pix'), may hold values from -1 to 4095, as said below
- analysis_fields: float32 [8, 8192], P(None, ('groups', 'pix')), parts along dimension 1, may hold values from -14.5 to 14.5
- depth_weight: float32 [9, 256], replicated, may hold values from -2 to 2
- norm_gain: float32 [256], replicated, may hold values from 0.5 to 2
- up_weight: bfloat16 [1024, 256], P('pix'), may hold values from -0.375 to 0.375
- up_bias: float32 [1024], replicated, may hold values from -3 to 3
- down_weight: bfloat16 [1024, 256], P('pix'), may hold values from -0.1875 to 0.1875
- layer_scale: float32 [256], replicated, may hold values from 0.25 to 1
- head_matrix: bfloat16 [8, 256], replicated, may hold values from -0.375 to 0.375
Outputs:
- mean_crps: float32 [2], P('groups'), parts along dimension 0
- input_grad: bfloat16 [2, 8192, 256], P('mem', ('groups', 'pix')), parts along dimension 1
- up_grad: float32 [2048, 256], P(('groups', 'pix')), parts along dimension 0
- down_grad: float32 [2048, 256], P(('groups', 'pix')), parts along dimension 0
- depth_grad: float32 [18, 256], P('groups'), parts along dimension 0
- head_grad: float32 [16, 256], P('groups'), parts along dimension 0
The draws below stay inside these ranges and needn't reach their ends.
There are 2 independent parts, one for each index of `groups`. The reference program is written for one: setup_inputs(seed, part) draws one part's arguments, and reference() takes and returns one part's arrays. A program takes and returns all parts, laid end to end along the dimension named above; an argument that names none is the same for every part. Nothing has to cross between parts.
Inputs may be any that keep to these rules, and one draw needn't show every extreme that they name: neighbours[t, p] is the pixel at tap t of pixel p; tap 4 is p itself. It lies in the same block of 512 consecutive pixels as p or in the block just before or after it. Taps mirror: wherever neighbours[t, p] = q >= 0, neighbours[8 - t, q] = p.
All inputs are finite; a program needn't handle non-finite values.
Results may differ from the reference program's by a relative error of at most 0.0095.
Values may be sent and summed in bfloat16 or wider, within the bound.
No kernel may reach another device: no remote copies, remote signals or barrier semaphores. Data moves between devices by JAX's collectives and lax.ppermute only.
A program may use at most 64 MiB of HBM per device.

```python
import math
import jax
import jax.numpy as jnp
from jax import lax

C = 256
FF = 1024
OUTPUT_FIELDS = 8
TAPS = 9
CYCLE = 256
PIXELS_PER_INDEX = 512
WINDOW_PIXELS = 4096
ENSEMBLE_SIZE = 2
N_PIX = 8


def draw_neighbours(key, part):
    key = jax.random.fold_in(key, 11)
    block_count = WINDOW_PIXELS // PIXELS_PER_INDEX
    orders = jax.vmap(lambda sub_key: jax.random.permutation(sub_key, PIXELS_PER_INDEX))(jax.random.split(key, block_count)).astype(jnp.int32)
    slot_of = jnp.argsort(orders, axis=1).astype(jnp.int32)
    natural = orders.reshape(-1)
    blocks = jnp.repeat(jnp.arange(block_count, dtype=jnp.int32), PIXELS_PER_INDEX)
    cycle_number = blocks * 2 + natural // CYCLE
    column = natural % CYCLE
    parity = cycle_number % 2
    cycle_steps = jnp.array([-2, -1, -1, 0, 0, 0, 1, 1, 2], jnp.int32)
    column_base = jnp.array([0, -1, 0, -1, 0, 1, -1, 0, 0], jnp.int32)
    column_parity = jnp.array([0, 1, 1, 0, 0, 0, 1, 1, 0], jnp.int32)
    near_cycle = cycle_number[None] + cycle_steps[:, None]
    near_column = column[None] + column_base[:, None] + column_parity[:, None] * parity[None]
    inside = (near_cycle >= 0) & (near_cycle < 2 * block_count) & (near_column >= 0) & (near_column < CYCLE)
    safe_cycle = jnp.clip(near_cycle, 0, 2 * block_count - 1)
    safe_column = jnp.clip(near_column, 0, CYCLE - 1)
    near_block = safe_cycle // 2
    near_natural = safe_cycle % 2 * CYCLE + safe_column
    near_slot = slot_of[near_block, near_natural]
    return jnp.where(inside, near_block * PIXELS_PER_INDEX + near_slot, -1).astype(jnp.int32)


def draw_analysis_fields(key, part):
    key = jax.random.fold_in(key, 23)
    position = jnp.arange(WINDOW_PIXELS, dtype=jnp.float32)[None, :] / WINDOW_PIXELS
    values = jnp.clip(jax.random.normal(key, (OUTPUT_FIELDS, WINDOW_PIXELS), jnp.float32), -4.0, 4.0)
    return (values * (1.0 + 2.0 * position)).astype(jnp.float32)


def block_levels(stream_key, extent, shards, low, top_value):
    def one(dim, shards_of):
        draws = jax.random.uniform(jax.random.fold_in(jax.random.fold_in(stream_key, 6), dim), (shards_of,), jnp.float32, low / len(shards), top_value / len(shards))
        return jnp.repeat(jnp.exp(draws), extent[dim] // shards_of).reshape((-1,) + (1,) * (len(extent) - dim - 1))

    factor_of = one(*shards[0])
    for cut in shards[1:]:
        factor_of = factor_of * one(*cut)
    return factor_of


def normal_values(rng, dims, deviation, reach, pieces=(), held_as=jnp.bfloat16):
    entries = jax.random.normal(rng, dims, jnp.float32) * deviation
    if len(pieces) > 0:
        entries = block_levels(rng, dims, pieces, -0.22, 0.18) * entries
    return jnp.clip(entries, min=-reach, max=reach).astype(held_as)


def setup_inputs(seed: int = 0, part: int = 0) -> dict:
    streams_of = jax.random.split(jax.random.key(seed), 11)
    part_splits = jax.random.split(jax.random.fold_in(streams_of[10], part), 11)
    return {
        "features": normal_values(part_splits[0], (ENSEMBLE_SIZE, WINDOW_PIXELS, C), 1.0, 6.0, ((0, 2), (1, 8))),
        "neighbours": draw_neighbours(jax.random.fold_in(streams_of[10], 71), part),
        "analysis_fields": draw_analysis_fields(jax.random.fold_in(jax.random.fold_in(streams_of[10], part), 71), part),
        "depth_weight": normal_values(streams_of[3], (TAPS, C), TAPS ** -0.5, 2.0, (), jnp.float32),
        "norm_gain": jnp.clip(jnp.exp(jax.random.uniform(streams_of[4], (C,), jnp.float32, math.log(0.5), math.log(2.0))), 0.5, 2.0),
        "up_weight": normal_values(streams_of[5], (FF, C), C ** -0.5, 0.375, ((0, 8),)),
        "up_bias": normal_values(streams_of[6], (FF,), 0.5, 3.0, (), jnp.float32),
        "down_weight": normal_values(streams_of[7], (FF, C), FF ** -0.5, 0.1875, ((0, 8),)),
        "layer_scale": jnp.clip(jnp.exp(jax.random.uniform(streams_of[8], (C,), jnp.float32, math.log(0.25), math.log(1.0))), 0.25, 1.0),
        "head_matrix": normal_values(streams_of[9], (OUTPUT_FIELDS, C), C ** -0.5, 0.375),
    }


def soft_abs(values):
    return jnp.sqrt(values * values + 0.04)

def slope_of(values):
    return values / soft_abs(values)

def gelu_value(values):
    return 0.5 * values * (1.0 + lax.erf(values * 0.7071067811865476))

def gelu_slope(values):
    return 0.5 * (1.0 + lax.erf(values * 0.7071067811865476)) + values * jnp.exp(-0.5 * values * values) * 0.3989422804014327

def ensemble_slopes(chosen, every, target_values):
    member_total = every.shape[0]
    direct = slope_of(chosen - target_values[None]) / member_total
    paired = lax.optimization_barrier(jnp.sum(slope_of(chosen[:, None] - every[None, :]), axis=1)) / (member_total * (member_total - 1.0))
    return (direct - paired).astype(jnp.bfloat16)

def fair_score_total(every, target_values):
    member_total = every.shape[0]
    pair_diff = every[:, None] - every[None, :]
    offdiag = (1.0 - jnp.eye(member_total, dtype=jnp.float32))[:, :, None, None]
    skill_term = lax.optimization_barrier(jnp.sum(soft_abs(every - target_values[None]), axis=0)) / member_total
    spread = lax.optimization_barrier(jnp.sum(soft_abs(pair_diff) * offdiag, axis=(0, 1))) / (2.0 * member_total * (member_total - 1))
    return jnp.sum(skill_term - spread)

def normalize(mixed, norm_gain):
    channel_mean = lax.optimization_barrier(jnp.mean(mixed, axis=-1, keepdims=True))
    centred = mixed - channel_mean
    inverse_deviation = lax.rsqrt(lax.optimization_barrier(jnp.mean(centred * centred, axis=-1, keepdims=True)) + 1e-06)
    scaled_values = centred * inverse_deviation
    return (scaled_values, inverse_deviation, (scaled_values * norm_gain).astype(jnp.bfloat16))

def norm_backward(normed_grad, scaled_values, inverse_deviation, norm_gain):
    gained = normed_grad * norm_gain
    centred = gained - lax.optimization_barrier(jnp.mean(gained, axis=-1, keepdims=True))
    return (inverse_deviation * (centred - scaled_values * lax.optimization_barrier(jnp.mean(gained * scaled_values, axis=-1, keepdims=True)))).astype(jnp.bfloat16)

def tap_gather(source, neighbour_table, tap_number):
    chosen = neighbour_table[tap_number]
    inside = (chosen >= 0).astype(jnp.float32)[None, :, None]
    return jnp.take(source, jnp.maximum(chosen, 0), axis=1).astype(jnp.float32) * inside

def tap_mix(source, neighbour_table, tap_weights):
    mixture = jnp.zeros((source.shape[0], neighbour_table.shape[1], source.shape[2]), jnp.float32)
    for tap_number in range(TAPS):
        mixture = mixture + tap_weights[tap_number] * tap_gather(source, neighbour_table, tap_number)
    return mixture

def block_forward(features, neighbours, depth_weight, norm_gain, up_weight, up_bias, down_weight, layer_scale, head_matrix, leading_pixel):
    neighbour_table = lax.dynamic_slice_in_dim(neighbours, leading_pixel, PIXELS_PER_INDEX, 1)
    own_features = lax.dynamic_slice_in_dim(features, leading_pixel, PIXELS_PER_INDEX, 1)
    mixed = tap_mix(features, neighbour_table, depth_weight)
    scaled_values, inverse_deviation, normed = normalize(mixed, norm_gain)
    normalized_rows = normed.reshape(-1, C)
    preactivation_values = jnp.dot(normalized_rows, up_weight.T, preferred_element_type=jnp.float32) + up_bias
    layer_activations = gelu_value(preactivation_values).astype(jnp.bfloat16)
    branch_sum = jnp.dot(layer_activations, down_weight, preferred_element_type=jnp.float32)
    carried_state = (own_features.astype(jnp.float32) + layer_scale * branch_sum.reshape(own_features.shape)).astype(jnp.bfloat16)
    member_prediction = jnp.einsum('hk,ftk->fht', head_matrix.astype(jnp.float32), carried_state.astype(jnp.float32))
    return (neighbour_table, scaled_values, inverse_deviation, normalized_rows, preactivation_values, layer_activations, carried_state, member_prediction)

def reference(features, neighbours, analysis_fields, depth_weight, norm_gain, up_weight, up_bias, down_weight, layer_scale, head_matrix):
    start_offsets = jnp.arange(N_PIX, dtype=jnp.int32) * PIXELS_PER_INDEX

    def inference_mode(leading_pixel):
        return block_forward(features, neighbours, depth_weight, norm_gain, up_weight, up_bias, down_weight, layer_scale, head_matrix, leading_pixel)[-1]
    prediction_blocks = lax.map(inference_mode, start_offsets)
    member_prediction = jnp.transpose(prediction_blocks, (1, 2, 0, 3)).reshape(ENSEMBLE_SIZE, OUTPUT_FIELDS, WINDOW_PIXELS)
    accumulated_loss = fair_score_total(member_prediction, analysis_fields)
    prediction_gradient = ensemble_slopes(member_prediction, member_prediction, analysis_fields)

    def backward_step(carry, leading_pixel):
        up_total, down_total, head_total, depth_total = carry
        output_values = block_forward(features, neighbours, depth_weight, norm_gain, up_weight, up_bias, down_weight, layer_scale, head_matrix, leading_pixel)
        neighbour_table, scaled_values, inverse_deviation, normalized_rows, preactivation_values, layer_activations, carried_state, discarded_prediction = output_values
        gradient_block = lax.dynamic_slice_in_dim(prediction_gradient, leading_pixel, PIXELS_PER_INDEX, 2).astype(jnp.float32)
        state_grad = jnp.einsum('rb,yrk->ykb', head_matrix.astype(jnp.float32), gradient_block)
        head_total = head_total + jnp.einsum('xjg,xgy->jy', gradient_block, carried_state.astype(jnp.float32))
        branch_grad = (layer_scale * state_grad).astype(jnp.bfloat16).reshape(-1, C)
        act_grad = jnp.dot(branch_grad, down_weight.T, preferred_element_type=jnp.float32)
        pre_grads = (act_grad * gelu_slope(preactivation_values)).astype(jnp.bfloat16)
        up_total = up_total + jnp.dot(pre_grads.T, normalized_rows, preferred_element_type=jnp.float32)
        down_total = down_total + jnp.dot(layer_activations.T, branch_grad, preferred_element_type=jnp.float32)
        normed_grad = jnp.dot(pre_grads, up_weight, preferred_element_type=jnp.float32)
        mixed_grad = norm_backward(normed_grad.reshape(scaled_values.shape), scaled_values, inverse_deviation, norm_gain)
        grad_float = mixed_grad.astype(jnp.float32)
        tap_terms = [lax.optimization_barrier(jnp.sum(tap_gather(features, neighbour_table, tap_number) * grad_float, axis=(0, 1))) for tap_number in range(TAPS)]
        depth_total = depth_total + jnp.stack(tap_terms)
        return ((up_total, down_total, head_total, depth_total), mixed_grad)
    initial = (jnp.zeros((FF, C), jnp.float32), jnp.zeros((FF, C), jnp.float32), jnp.zeros((OUTPUT_FIELDS, C), jnp.float32), jnp.zeros((TAPS, C), jnp.float32))
    totals, grad_blocks = lax.scan(backward_step, initial, start_offsets)
    up_total, down_total, head_total, depth_total = totals
    mixed_grad_all = jnp.transpose(grad_blocks, (1, 0, 2, 3)).reshape(ENSEMBLE_SIZE, WINDOW_PIXELS, C)

    def input_block(leading_pixel):
        neighbour_table = lax.dynamic_slice_in_dim(neighbours, leading_pixel, PIXELS_PER_INDEX, 1)
        gradient_block = lax.dynamic_slice_in_dim(prediction_gradient, leading_pixel, PIXELS_PER_INDEX, 2).astype(jnp.float32)
        state_grad = jnp.einsum('rb,yrk->ykb', head_matrix.astype(jnp.float32), gradient_block)
        return (state_grad + tap_mix(mixed_grad_all, neighbour_table, depth_weight[::-1])).astype(jnp.bfloat16)
    input_blocks = lax.map(input_block, start_offsets)
    input_grad = jnp.transpose(input_blocks, (1, 0, 2, 3)).reshape(ENSEMBLE_SIZE, WINDOW_PIXELS, C)
    grad_scale = 1.0 / math.sqrt(WINDOW_PIXELS * ENSEMBLE_SIZE)
    mean_crps = (accumulated_loss / (WINDOW_PIXELS * OUTPUT_FIELDS)).reshape(1)
    return (mean_crps, input_grad, up_total * grad_scale, down_total * grad_scale, depth_total * grad_scale, head_total * grad_scale)
```

```python
import math

import jax
import jax.numpy as jnp
from jax import lax
from jax.experimental import pallas as pl
from jax.experimental.pallas import tpu as pltpu
from jax.sharding import PartitionSpec as P

F32 = jnp.float32
BF16 = jnp.bfloat16
LANES = 128
EXTRA = 48
NN = (((1,), (0,)), ((), ()))
NT = (((1,), (1,)), ((), ()))
TN = (((0,), (0,)), ((), ()))


def mul(a, b, dims=NN):
    return lax.dot_general(a, b, dims, preferred_element_type=F32)


def params(mib):
    return pltpu.CompilerParams(vmem_limit_bytes=mib * 2**20)


def halves(values):
    high = values.astype(BF16)
    return high, (values - high.astype(F32)).astype(BF16)


def tap_rows(places, extended, tap):
    rows, count = places.shape[0], extended.shape[0]
    column = lax.broadcasted_iota(jnp.int32, (rows, count), 1)
    chosen = (column == places[:, tap : tap + 1]).astype(F32).astype(BF16)
    return mul(chosen, extended)


def row_mean(values):
    return jnp.mean(values, axis=-1, keepdims=True)


def mix_kernel(before, own, after, places, weights, gain, taken, mixed_out, normed_out):
    extended = jnp.concatenate([before[...], own[...], after[...]], axis=0)
    where = places[...]
    mixed = jnp.zeros(own.shape, F32)
    for tap in range(weights.shape[0]):
        rows = tap_rows(where, extended, tap)
        taken[tap] = rows.astype(BF16)
        mixed = mixed + weights[tap : tap + 1, :] * rows
    mixed_out[...] = mixed
    centred = mixed - row_mean(mixed)
    inverse = lax.rsqrt(row_mean(centred * centred) + 1e-06)
    normed_out[...] = (centred * inverse * gain[...]).astype(BF16)


def forward_kernel(
    normed, up, bias, down, scale, head, features, act_out, slope_out, reach_out, forecast_out
):
    weighed = head[...].astype(F32) * scale[...]
    high, low = halves(weighed)
    reach = mul(jnp.concatenate([high, low], axis=0), down[...], NT)
    reach = reach[:8] + reach[8:]
    high, low = halves(reach)
    both = jnp.concatenate([high, low], axis=0)
    reach_out[...] = both
    rows = normed[...]
    total = mul(head[...], features[...], NT)
    hidden = up.shape[0]
    for low_edge in range(0, hidden, 256):
        piece = slice(low_edge, low_edge + 256)
        pre = mul(rows, up[piece, :], NT) + bias[:, piece]
        phi = 0.5 + 0.5 * lax.erf(pre * 0.7071067811865476)
        act = (pre * phi).astype(BF16)
        act_out[:, piece] = act
        slope_out[:, piece] = phi + pre * jnp.exp(-0.5 * pre * pre) * 0.3989422804014327
        part = mul(both[:, piece], act, NT)
        total = total + part[:8] + part[8:]
    forecast_out[...] = total


def soft_abs(values):
    return jnp.sqrt(values * values + 0.04)


def backward_kernel(
    mine, other, target, reach, slope, up, mixed, gain, mixed_grad, pre_out, grad_out, loss_out
):
    apart = mine[...] - target[...]
    spread = mine[...] - other[...]
    apart_abs, spread_abs = soft_abs(apart), soft_abs(spread)
    grad = (0.5 * (apart / apart_abs) - 0.5 * (spread / spread_abs)).astype(BF16)
    grad_out[...] = grad
    loss = jnp.sum(0.5 * apart_abs - 0.25 * spread_abs)
    loss_out[...] = jnp.full(loss_out.shape, loss, F32)
    twice = jnp.concatenate([grad.astype(F32), grad.astype(F32)], axis=0).T.astype(BF16)
    normed_grad = jnp.zeros(mixed.shape, F32)
    for low_edge in range(0, up.shape[0], 256):
        piece = slice(low_edge, low_edge + 256)
        act_grad = mul(twice, reach[:, piece])
        pre = (act_grad * slope[:, piece]).astype(BF16)
        pre_out[:, piece] = pre
        normed_grad = normed_grad + mul(pre, up[piece, :])
    values = mixed[...]
    centred = values - row_mean(values)
    inverse = lax.rsqrt(row_mean(centred * centred) + 1e-06)
    z = centred * inverse
    gained = normed_grad * gain[...]
    mixed_grad[...] = (
        inverse * (gained - row_mean(gained) - z * row_mean(gained * z))
    ).astype(BF16)


def weights_kernel(
    pre_grad, normed, act, grad, features, down, scale, taken, mixed_grad, loss, pay
):
    blocks = pay.shape[1]
    normed_t = normed[...].astype(F32).T.astype(BF16)
    summed = mul(grad[...], act[...])
    high, low = halves(summed)
    through = mul(jnp.concatenate([high, low], axis=0), down[...])
    head_part = mul(grad[...], features[...]) + scale[...] * (through[:8] + through[8:])
    flow = mixed_grad[...].astype(F32)
    depth = [
        jnp.sum(taken[tap].astype(F32) * flow, axis=0, keepdims=True)
        for tap in range(taken.shape[0])
    ]
    small = jnp.concatenate([head_part] + depth, axis=0)
    for block in range(blocks):
        lanes = slice(block * LANES, (block + 1) * LANES)
        up_part = mul(normed_t, pre_grad[:, lanes])
        for half in range(2):
            pay[half, block, :LANES, :] = up_part[half * LANES : (half + 1) * LANES].astype(BF16)
            extra = jnp.concatenate(
                [
                    small[:, half * LANES : (half + 1) * LANES],
                    loss[...],
                    summed[4 * half : 4 * half + 4, lanes],
                    jnp.zeros((2, LANES), F32),
                ],
                axis=0,
            )
            high, low = halves(extra)
            pay[half, block, LANES:, :] = jnp.concatenate([high, low], axis=0)


def input_kernel(before, own, after, places, weights, grad, head, out):
    extended = jnp.concatenate([before[...], own[...], after[...]], axis=0)
    where = places[...]
    taps = weights.shape[0]
    total = mul(grad[...].astype(F32).T.astype(BF16), head[...])
    for tap in range(taps):
        total = total + weights[taps - 1 - tap : taps - tap, :] * tap_rows(where, extended, tap)
    out[...] = total.astype(BF16)


def call(kernel, outs, mib, *operands):
    return pl.pallas_call(
        kernel,
        out_shape=tuple(jax.ShapeDtypeStruct(shape, dtype) for shape, dtype in outs),
        compiler_params=params(mib),
    )(*operands)


def neighbour_blocks(array):
    count = lax.axis_size("pix")
    up = [(i, i + 1) for i in range(count - 1)]
    down = [(j, i) for i, j in up]
    return lax.ppermute(array, "pix", up), lax.ppermute(array, "pix", down)


def swap(array):
    return lax.ppermute(array, "mem", [(0, 1), (1, 0)])


def gather_weights(up_weight, down_weight, member):
    count, rows = lax.axis_size("pix"), up_weight.shape[0]
    if rows % 32 != 0:
        return (
            lax.all_gather(up_weight, "pix", axis=0, tiled=True),
            lax.all_gather(down_weight, "pix", axis=0, tiled=True),
        )
    both = jnp.stack([up_weight, down_weight])
    half = rows // 2
    mine = lax.dynamic_slice_in_dim(both, member * half, half, 1)
    mine = jnp.broadcast_to(mine[None], (count,) + mine.shape)
    mine = lax.all_to_all(mine, "pix", split_axis=0, concat_axis=0)
    other = swap(mine)
    first = jnp.where(member == 0, mine, other)
    second = jnp.where(member == 0, other, mine)
    whole = jnp.stack([first, second], axis=2)
    return whole[:, 0].reshape(count * rows, -1), whole[:, 1].reshape(count * rows, -1)


def local(
    features,
    neighbours,
    analysis_fields,
    depth_weight,
    norm_gain,
    up_weight,
    up_bias,
    down_weight,
    layer_scale,
    head_matrix,
):
    pixels, channels = features.shape[1:]
    count = lax.axis_size("pix")
    owned_rows = up_weight.shape[0]
    hidden = owned_rows * count
    taps = neighbours.shape[0]
    position, member = lax.axis_index("pix"), lax.axis_index("mem")
    own = features[0]
    gain, scale, bias = norm_gain[None], layer_scale[None], up_bias[None]
    places = jnp.where(neighbours >= 0, neighbours - (position - 1) * pixels, -1).T

    before, after = neighbour_blocks(own)
    up, down = gather_weights(up_weight, down_weight, member)
    taken, mixed, normed = call(
        mix_kernel,
        [((taps, pixels, channels), BF16), ((pixels, channels), F32), ((pixels, channels), BF16)],
        40,
        before, own, after, places, depth_weight, gain,
    )
    act, slope, reach, forecast = call(
        forward_kernel,
        [((pixels, hidden), BF16), ((pixels, hidden), F32), ((16, hidden), BF16), ((8, pixels), F32)],
        40,
        normed, up, bias, down, scale, head_matrix, own,
    )
    other = swap(forecast)
    mixed_grad, pre_grad, grad, loss = call(
        backward_kernel,
        [((pixels, channels), BF16), ((pixels, hidden), BF16), ((8, pixels), BF16), ((1, LANES), F32)],
        40,
        forecast, other, analysis_fields, reach, slope, up, mixed, gain,
    )
    grad_before, grad_after = neighbour_blocks(mixed_grad)
    (pay,) = call(
        weights_kernel,
        [((2, hidden // LANES, LANES + EXTRA, LANES), BF16)],
        40,
        pre_grad, normed, act, grad, own, down, scale, taken, mixed_grad, loss,
    )
    (input_grad,) = call(
        input_kernel,
        [((pixels, channels), BF16)],
        40,
        grad_before, mixed_grad, grad_after, places, depth_weight, grad, head_matrix,
    )
    grad_scale = 1.0 / math.sqrt(pixels * count * 2)
    keep = lax.dynamic_index_in_dim(pay, member, 0, keepdims=False)
    send = lax.dynamic_index_in_dim(pay, 1 - member, 0, keepdims=False)
    block_rows = EXTRA // 2
    joined = (keep.astype(F32) + swap(send).astype(F32))
    fine = joined[:, LANES : LANES + block_rows] + joined[:, LANES + block_rows :]
    if owned_rows == LANES:
        high, low = halves(fine)
        joined = jnp.concatenate([joined[:, :LANES].astype(BF16), high, low], axis=1)
        joined = lax.all_to_all(joined, "pix", split_axis=0, concat_axis=0)
        total = jnp.sum(joined.astype(F32), axis=0)
        total = jnp.concatenate(
            [total[:LANES], total[LANES : LANES + block_rows] + total[LANES + block_rows :]], axis=0
        )
        ours, theirs = total, swap(total)
        first = jnp.where(member == 0, ours, theirs)
        second = jnp.where(member == 0, theirs, ours)
        up_grad = jnp.concatenate([first[:LANES], second[:LANES]], axis=0).T
        small = jnp.concatenate([first[LANES:], second[LANES:]], axis=1)
        summed = jnp.concatenate([first[LANES + 18 : LANES + 22], second[LANES + 18 : LANES + 22]])
    else:
        pair = jnp.stack([joined[:, :LANES], swap(joined[:, :LANES])])
        pair = jnp.where(member == 0, pair, pair[::-1])
        rows = jnp.transpose(pair, (1, 3, 0, 2)).reshape(hidden, channels)
        up_grad = lax.psum_scatter(rows, "pix", scatter_dimension=0, tiled=True)
        fine_pair = jnp.stack([fine, swap(fine)])
        fine_pair = jnp.where(member == 0, fine_pair, fine_pair[::-1])
        small = jnp.transpose(fine_pair[:, 0], (1, 0, 2)).reshape(block_rows, channels)
        small = lax.psum(small, "pix")
        summed = jnp.transpose(fine_pair[:, :, 18:22], (1, 3, 0, 2)).reshape(hidden, 8)
        summed = lax.psum_scatter(summed, "pix", scatter_dimension=0, tiled=True).T
    down_grad = layer_scale * lax.dot_general(
        summed, head_matrix.astype(F32), TN, precision=lax.Precision.HIGHEST
    )
    mean_crps = (small[17, 0] / (pixels * count * 8)).reshape(1)
    return (
        mean_crps,
        input_grad[None],
        up_grad * grad_scale,
        down_grad * grad_scale,
        small[8 : 8 + taps] * grad_scale,
        small[:8] * grad_scale,
    )


def solution(mesh):
    return jax.shard_map(
        local,
        mesh=mesh,
        in_specs=(
            P("mem", ("groups", "pix"), None),
            P(None, "pix"),
            P(None, ("groups", "pix")),
            P(),
            P(),
            P("pix", None),
            P(),
            P("pix", None),
            P(),
            P(),
        ),
        out_specs=(
            P("groups"),
            P("mem", ("groups", "pix"), None),
            P(("groups", "pix"), None),
            P(("groups", "pix"), None),
            P("groups", None),
            P("groups", None),
        ),
        check_vma=False,
    )
```

```python
import functools
import math

import jax
import jax.numpy as jnp
from jax import lax
from jax.experimental import pallas as pl
from jax.experimental.pallas import tpu as pltpu
from jax.sharding import PartitionSpec as P

F32 = jnp.float32
BF16 = jnp.bfloat16
LANES = 128
EXTRA = 48
CENTRE = 4
NN = (((1,), (0,)), ((), ()))
NT = (((1,), (1,)), ((), ()))
TN = (((0,), (0,)), ((), ()))
FAR = -1e6
NEAR = 50 * 10**9
OWN = 8 * 10**9


def mul(a, b, dims=NN):
    return lax.dot_general(a, b, dims, preferred_element_type=F32)


def halves(values):
    high = values.astype(BF16)
    return high, (values - high.astype(F32)).astype(BF16)


def row_mean(values):
    return jnp.mean(values, axis=-1, keepdims=True)


def soft_abs(values):
    return jnp.sqrt(values * values + 0.04)


def turned(values):
    return values.astype(F32).T.astype(BF16)


def relative_places(info, neighbours):
    table = neighbours[...]
    relative = jnp.where(table >= 0, (table - info[0]).astype(F32), FAR)
    fill = jnp.full((16 - table.shape[0], table.shape[1]), FAR, F32)
    return jnp.concatenate([relative, fill], axis=0).T


def pair_places(info, neighbours):
    pixels = neighbours.shape[1]
    return relative_places(info, neighbours) + jnp.where(info[1] == 0, -pixels, pixels).astype(F32)


def side_places(info, neighbours):
    pixels = neighbours.shape[1]
    return relative_places(info, neighbours) + jnp.where(info[1] == 0, pixels, -pixels).astype(F32)


def tap_rows(places, source, tap):
    column = lax.broadcasted_iota(jnp.int32, (places.shape[0], source.shape[0]), 1).astype(F32)
    chosen = jnp.where(column == places[:, tap : tap + 1], 1.0, 0.0).astype(BF16)
    return mul(chosen, source)


def load(pairs, sems):
    copies = [pltpu.make_async_copy(src, dst, sems.at[k]) for k, (src, dst) in enumerate(pairs)]
    for copy in copies:
        copy.start()
    for copy in copies:
        copy.wait()


def spread_kernel(rows, out):
    for owner in range(out.shape[0]):
        out[owner] = rows[...]


def mix_own_kernel(
    info, own_hbm, neighbours_hbm, weights_hbm, head_hbm, scale_hbm, gain_hbm, bias_hbm, target_hbm,
    own, weights, head, scale, gain, bias, target,
    neighbours, taken, mixed_out, base_out, sems,
):
    load(
        [(own_hbm, own), (neighbours_hbm, neighbours), (weights_hbm, weights), (head_hbm, head),
         (scale_hbm, scale), (gain_hbm, gain), (bias_hbm, bias), (target_hbm, target)],
        sems,
    )
    source = own[...]
    places = relative_places(info, neighbours)
    base_out[...] = mul(head[...], source, NT)
    mixed = weights[CENTRE : CENTRE + 1, :] * source.astype(F32)
    for tap in range(weights.shape[0]):
        if tap != CENTRE:
            rows = tap_rows(places, source, tap)
            taken[tap - (tap > CENTRE)] = rows.astype(BF16)
            mixed = mixed + weights[tap : tap + 1, :] * rows
    mixed_out[...] = mixed


def mix(where, tile, weights, mixed_in, taken, mixed_out):
    source = tile[...]
    mixed = mixed_in[...]
    for tap in range(weights.shape[0]):
        if tap != CENTRE:
            rows = tap_rows(where, source, tap)
            taken[tap - (tap > CENTRE)] = rows.astype(BF16)
            mixed = mixed + weights[tap : tap + 1, :] * rows
    mixed_out[...] = mixed


def mix_pair_kernel(info, tile, neighbours, weights, mixed_in, taken, mixed_out):
    mix(pair_places(info, neighbours), tile, weights, mixed_in, taken, mixed_out)


def mix_side_kernel(
    info, tile, neighbours, weights, gain, mixed_in, taken, mixed_out, normed_out
):
    mix(side_places(info, neighbours), tile, weights, mixed_in, taken, mixed_out)
    mixed = mixed_out[...]
    centred = mixed - row_mean(mixed)
    inverse = lax.rsqrt(row_mean(centred * centred) + 1e-06)
    normed_out[...] = (centred * inverse * gain[...]).astype(BF16)


def forward_kernel(
    info, normed, mine, other, bias, base, head, scale,
    act_out, slope_out, forecast_out, up, down, reach,
):
    owners = mine.shape[0]
    half = mine.shape[1] // 2
    for owner in range(owners):
        for side in range(2):
            rows = slice((2 * owner + side) * half, (2 * owner + side + 1) * half)
            up[rows, :] = jnp.where(info[2] == side, mine[owner, :half], other[owner, :half])
            down[rows, :] = jnp.where(info[2] == side, mine[owner, half:], other[owner, half:])
    high, low = halves(head[...].astype(F32) * scale[...])
    product = mul(jnp.concatenate([high, low], axis=0), down[...], NT)
    high, low = halves(product[:8] + product[8:])
    reach[...] = jnp.concatenate([high, low], axis=0)
    forward(normed, up, reach, bias, base, act_out, slope_out, forecast_out)


def forward(normed, up, reach, bias, base, act_out, slope_out, forecast_out):
    rows = normed[...]
    total = base[...]
    for low_edge in range(0, up.shape[0], 256):
        piece = slice(low_edge, low_edge + 256)
        pre = mul(rows, up[piece, :], NT) + bias[:, piece]
        phi = 0.5 + 0.5 * lax.erf(pre * 0.7071067811865476)
        act = (pre * phi).astype(BF16)
        act_out[:, piece] = act
        slope_out[:, piece] = phi + pre * jnp.exp(-0.5 * pre * pre) * 0.3989422804014327
        part = mul(reach[:, piece], act, NT)
        total = total + part[:8] + part[8:]
    forecast_out[...] = total


def backward_kernel(
    mine, other, target, reach, slope, up, mixed, gain, mixed_grad, pre_out, grad_out, loss_out
):
    apart = mine[...] - target[...]
    spread = mine[...] - other[...]
    apart_abs, spread_abs = soft_abs(apart), soft_abs(spread)
    grad = (0.5 * (apart / apart_abs) - 0.5 * (spread / spread_abs)).astype(BF16)
    grad_out[...] = grad
    loss_out[...] = jnp.full(loss_out.shape, jnp.sum(0.5 * apart_abs - 0.25 * spread_abs), F32)
    twice = turned(jnp.concatenate([grad, grad], axis=0))
    normed_grad = jnp.zeros(mixed.shape, F32)
    for low_edge in range(0, up.shape[0], 256):
        piece = slice(low_edge, low_edge + 256)
        pre = (mul(twice, reach[:, piece]) * slope[:, piece]).astype(BF16)
        pre_out[:, piece] = pre
        normed_grad = normed_grad + mul(pre, up[piece, :])
    values = mixed[...]
    centred = values - row_mean(values)
    inverse = lax.rsqrt(row_mean(centred * centred) + 1e-06)
    z = centred * inverse
    gained = normed_grad * gain[...]
    mixed_grad[...] = (
        inverse * (gained - row_mean(gained) - z * row_mean(gained * z))
    ).astype(BF16)


def weights_kernel(
    info, pre_grad, normed, act, grad, features, down, scale, a, b, c, mixed_grad, loss,
    keep, send, small,
):
    normed_t = turned(normed[...])
    summed = mul(grad[...], act[...])
    high, low = halves(summed)
    through = mul(jnp.concatenate([high, low], axis=0), down[...])
    head_part = mul(grad[...], features[...]) + scale[...] * (through[:8] + through[8:])
    flow = mixed_grad[...].astype(F32)
    depth = [
        jnp.sum((a[k] + b[k] + c[k]).astype(F32) * flow, axis=0, keepdims=True)
        for k in range(a.shape[0])
    ]
    depth.insert(CENTRE, jnp.sum(features[...].astype(F32) * flow, axis=0, keepdims=True))
    small[...] = jnp.concatenate([head_part] + depth + [loss[...]], axis=0)
    first = info[2] == 0
    for block in range(keep.shape[0]):
        lanes = slice(block * LANES, (block + 1) * LANES)
        up_part = mul(normed_t, pre_grad[:, lanes])
        lower, higher = up_part[:LANES], up_part[LANES:]
        keep[block, :LANES, :] = jnp.where(first, lower, higher).astype(BF16)
        send[block, :, :] = jnp.where(first, higher, lower).astype(BF16)
        extra = [small[:, :LANES], small[:, LANES:], summed[:, lanes], jnp.zeros((4, LANES), F32)]
        keep[block, LANES:, :] = jnp.concatenate(extra, axis=0).astype(BF16)


def join_kernel(keep, came, joined):
    for block in range(keep.shape[0]):
        main = keep[block, :LANES, :].astype(F32) + came[block].astype(F32)
        joined[block, :LANES, :] = main.astype(BF16)
        joined[block, LANES:, :] = keep[block, LANES:, :]


def sum_kernel(parts, total):
    value = parts[0].astype(F32)
    for part in range(1, parts.shape[0]):
        value = value + parts[part].astype(F32)
    total[...] = value


def final_kernel(factors, info, ours, theirs, head, scale, mean, up, down, depth, head_out):
    loss_factor, factor = factors
    mine, other = ours[:LANES, :], theirs[:LANES, :]
    up[:, :LANES] = jnp.where(info[2] == 0, mine, other).T * factor
    up[:, LANES:] = jnp.where(info[2] == 0, other, mine).T * factor
    extra = ours[LANES:, :] + theirs[LANES:, :]
    small = jnp.concatenate([extra[:18], extra[18:36]], axis=1)
    head_out[...] = small[:8] * factor
    depth[...] = small[8:17] * factor
    mean[0] = jnp.sum(small[17:18, :1]) * loss_factor
    high, low = halves(extra[36:44])
    turn = jnp.concatenate([high, low], axis=0).astype(F32).T.astype(BF16)
    down[...] = mul(turn, jnp.concatenate([head[...], head[...]], axis=0)) * (scale[...] * factor)


def back_taps(total, source, places, weights):
    last = weights.shape[0] - 1
    for tap in range(last + 1):
        if tap != CENTRE:
            total = total + weights[last - tap : last - tap + 1, :] * tap_rows(places, source, tap)
    return total


def input_own_kernel(info, own, neighbours, weights, grad, head, out):
    source = own[...]
    centre = weights.shape[0] - 1 - CENTRE
    total = mul(turned(grad[...]), head[...])
    total = total + weights[centre : centre + 1, :] * source.astype(F32)
    out[...] = back_taps(total, source, relative_places(info, neighbours), weights)


def input_pair_kernel(info, tile, neighbours, weights, partial, out):
    out[...] = back_taps(partial[...], tile[...], pair_places(info, neighbours), weights)


def input_side_kernel(info, tile, neighbours, weights, partial, out):
    total = back_taps(partial[...], tile[...], side_places(info, neighbours), weights)
    out[...] = total.astype(BF16)


def call(
    kernel, outs, scalars, *operands, hbm=0, scratch=(), aliases=None, flops=2000000000, mib=8, smem_outs=(), last=False
):
    smem = pl.BlockSpec(memory_space=pltpu.SMEM)
    out_spec = pl.BlockSpec() if last else pl.BlockSpec(memory_space=pltpu.VMEM)
    kinds = [smem] * scalars + [pl.BlockSpec(memory_space=pltpu.HBM)] * hbm
    kinds = kinds + [pl.BlockSpec()] * (len(operands) - len(kinds))
    return pl.pallas_call(
        kernel,
        out_shape=tuple(jax.ShapeDtypeStruct(shape, dtype) for shape, dtype in outs),
        in_specs=kinds,
        out_specs=tuple(smem if k in smem_outs else out_spec for k in range(len(outs))),
        scratch_shapes=list(scratch),
        input_output_aliases=aliases or {},
        compiler_params=pltpu.CompilerParams(vmem_limit_bytes=mib * 2**20),
        cost_estimate=pl.CostEstimate(flops=flops, bytes_accessed=0, transcendentals=0),
    )(*operands)


def pair_tiles(array):
    count = lax.axis_size("pix")
    inner = [(i, i ^ 1) for i in range(count)]
    outer = [(i, i + 1) for i in range(1, count - 1, 2)]
    outer = outer + [(j, i) for i, j in outer]
    return lax.ppermute(array, "pix", inner), lax.ppermute(array, "pix", outer)


def swap(array):
    return lax.ppermute(array, "mem", [(0, 1), (1, 0)])


def local(
    features,
    neighbours,
    analysis_fields,
    depth_weight,
    norm_gain,
    up_weight,
    up_bias,
    down_weight,
    layer_scale,
    head_matrix,
):
    pixels, channels = features.shape[1:]
    count = lax.axis_size("pix")
    owned_rows = up_weight.shape[0]
    hidden = owned_rows * count
    taps = neighbours.shape[0]
    position, member = lax.axis_index("pix"), lax.axis_index("mem")
    info = jnp.stack([position * pixels, position % 2, member]).astype(jnp.int32)
    own = features[0]
    gain, scale, bias = norm_gain[None], layer_scale[None], up_bias[None]
    by_blocks = owned_rows == LANES
    exact = lax.Precision.HIGHEST
    tile, many = (pixels, channels), (taps - 1, pixels, channels)

    def everywhere(array):
        return lax.all_to_all(array, "pix", split_axis=0, concat_axis=0)

    pair, side = pair_tiles(own)
    if by_blocks:
        half = owned_rows // 2
        rows = jnp.stack([up_weight, down_weight])
        rows = lax.dynamic_slice_in_dim(rows, member * half, half, 1)
        (rows,) = call(
            spread_kernel,
            [((count, owned_rows, channels), BF16)],
            0,
            rows.reshape(owned_rows, channels),
            flops=OWN,
        )
        mine = everywhere(rows)
    else:
        up = lax.all_gather(up_weight, "pix", axis=0, tiled=True)
        down = lax.all_gather(down_weight, "pix", axis=0, tiled=True)
        reach = lax.dot_general(
            head_matrix.astype(F32) * layer_scale, down.astype(F32), NT, precision=exact
        )
        reach = jnp.concatenate(halves(reach), axis=0)
    own, weights, head, scale, gain, bias, target, places, taken, mixed, base = call(
        mix_own_kernel,
        [(tile, BF16), (depth_weight.shape, F32), (head_matrix.shape, BF16),
         ((1, channels), F32), ((1, channels), F32), ((1, hidden), F32), ((8, pixels), F32),
         (neighbours.shape, jnp.int32), (many, BF16), (tile, F32), ((8, pixels), F32)],
        1,
        info, own, neighbours, depth_weight, head_matrix, scale, gain, bias, analysis_fields,
        hbm=8,
        scratch=[pltpu.SemaphoreType.DMA((8,))],
        flops=OWN,
    )
    taken_pair, mixed = call(
        mix_pair_kernel,
        [(many, BF16), (tile, F32)],
        1,
        info, pair, places, weights, mixed,
        flops=NEAR,
    )
    taken_side, mixed, normed = call(
        mix_side_kernel,
        [(many, BF16), (tile, F32), (tile, BF16)],
        1,
        info, side, places, weights, gain, mixed,
        flops=NEAR,
    )
    outs = [((pixels, hidden), BF16), ((pixels, hidden), F32), ((8, pixels), F32)]
    if by_blocks:
        mine, normed = lax.optimization_barrier((mine, normed))
        other = swap(mine)
        whole = ((hidden, channels), BF16)
        act, slope, forecast, up, down, reach = call(
            forward_kernel,
            outs + [whole, whole, ((16, hidden), BF16)],
            1,
            info, normed, mine, other, bias, base, head, scale,
        )
    else:
        act, slope, forecast = call(forward, outs, 0, normed, up, reach, bias, base)
    mixed_grad, pre_grad, grad, loss = call(
        backward_kernel,
        [(tile, BF16), ((pixels, hidden), BF16), ((8, pixels), BF16), ((1, channels), F32)],
        0,
        forecast, swap(forecast), target, reach, slope, up, mixed, gain,
    )
    blocks = hidden // LANES
    full = ((blocks, LANES + EXTRA, LANES), BF16)
    keep, send, small = call(
        weights_kernel,
        [full, ((blocks, LANES, LANES), BF16), ((18, channels), F32)],
        1,
        info, pre_grad, normed, act, grad, own, down, scale, taken, taken_pair, taken_side,
        mixed_grad, loss,
        flops=NEAR,
    )
    came = swap(send)
    grad_pair, grad_side = pair_tiles(mixed_grad)
    (joined,) = call(join_kernel, [full], 0, keep, came)
    source, joined = lax.optimization_barrier((mixed_grad, joined))
    (partial,) = call(
        input_own_kernel, [(tile, F32)], 1, info, source, places, weights, grad, head, flops=OWN
    )
    (partial,) = call(
        input_pair_kernel,
        [(tile, F32)],
        1,
        info, grad_pair, places, weights, partial,
        flops=NEAR,
    )
    (input_grad,) = call(
        input_side_kernel,
        [(tile, BF16)],
        1,
        info, grad_side, places, weights, partial,
        flops=NEAR,
        last=True,
    )
    grad_scale = 1.0 / math.sqrt(pixels * count * 2)
    loss_scale = 1.0 / (pixels * count * 8)
    if by_blocks:
        parts, input_grad = lax.optimization_barrier((everywhere(joined), input_grad))
        (total,) = call(sum_kernel, [((LANES + EXTRA, LANES), F32)], 0, parts)
        mean_crps, up_grad, down_grad, depth_grad, head_grad = call(
            functools.partial(final_kernel, (loss_scale, grad_scale)),
            [((1,), F32), ((LANES, channels), F32), ((LANES, channels), F32),
             ((taps, channels), F32), ((8, channels), F32)],
            1,
            info, total, swap(total), head, scale,
            smem_outs=(0,),
            last=True,
        )
        return mean_crps, input_grad[None], up_grad, down_grad, depth_grad, head_grad

    main = joined[:, :LANES].astype(F32)
    main = jnp.stack([main, swap(main)])
    main = jnp.where(member == 0, main, main[::-1])
    rows = jnp.transpose(main, (1, 3, 0, 2)).reshape(hidden, channels)
    up_grad = lax.psum_scatter(rows, "pix", scatter_dimension=0, tiled=True)
    summed = keep[:, LANES + 36 : LANES + 44].astype(F32)
    summed = jnp.transpose(summed + swap(summed), (0, 2, 1)).reshape(hidden, 8)
    summed = lax.psum_scatter(summed, "pix", scatter_dimension=0, tiled=True)
    down_grad = layer_scale * jnp.dot(summed, head_matrix.astype(F32), precision=exact)
    small = lax.psum(small, ("pix", "mem"))
    return (
        small[17, :1] * loss_scale,
        input_grad[None],
        up_grad * grad_scale,
        down_grad * grad_scale,
        small[8:17] * grad_scale,
        small[:8] * grad_scale,
    )


def solution(mesh):
    return jax.shard_map(
        local,
        mesh=mesh,
        in_specs=(
            P("mem", ("groups", "pix"), None),
            P(None, "pix"),
            P(None, ("groups", "pix")),
            P(),
            P(),
            P("pix", None),
            P(),
            P("pix", None),
            P(),
            P(),
        ),
        out_specs=(
            P("groups"),
            P("mem", ("groups", "pix"), None),
            P(("groups", "pix"), None),
            P(("groups", "pix"), None),
            P("groups", None),
            P("groups", None),
        ),
        check_vma=False,
    )
```

```python
import functools
import math

import jax
import jax.numpy as jnp
from jax import lax
from jax.experimental import pallas as pl
from jax.experimental.pallas import tpu as pltpu
from jax.sharding import PartitionSpec as P

F32 = jnp.float32
BF16 = jnp.bfloat16
LANES = 128
EXTRA = 48
CENTRE = 4
NN = (((1,), (0,)), ((), ()))
NT = (((1,), (1,)), ((), ()))
TN = (((0,), (0,)), ((), ()))
FAR = -1e6
NEAR = 50 * 10**9
OWN = 8 * 10**9


def mul(a, b, dims=NN):
    return lax.dot_general(a, b, dims, preferred_element_type=F32)


def halves(values):
    high = values.astype(BF16)
    return high, (values - high.astype(F32)).astype(BF16)


def row_mean(values):
    return jnp.mean(values, axis=-1, keepdims=True)


def soft_abs(values):
    return jnp.sqrt(values * values + 0.04)


def turned(values):
    return values.astype(F32).T.astype(BF16)


def relative_places(info, neighbours):
    table = neighbours[...]
    relative = jnp.where(table >= 0, (table - info[0]).astype(F32), FAR)
    fill = jnp.full((16 - table.shape[0], table.shape[1]), FAR, F32)
    return jnp.concatenate([relative, fill], axis=0).T


def pair_places(info, neighbours):
    pixels = neighbours.shape[1]
    return relative_places(info, neighbours) + jnp.where(info[1] == 0, -pixels, pixels).astype(F32)


def side_places(info, neighbours):
    pixels = neighbours.shape[1]
    return relative_places(info, neighbours) + jnp.where(info[1] == 0, pixels, -pixels).astype(F32)


def tap_rows(places, source, tap):
    column = lax.broadcasted_iota(jnp.int32, (places.shape[0], source.shape[0]), 1).astype(F32)
    chosen = jnp.where(column == places[:, tap : tap + 1], 1.0, 0.0).astype(BF16)
    return mul(chosen, source)


def load(pairs, sems):
    copies = [pltpu.make_async_copy(src, dst, sems.at[k]) for k, (src, dst) in enumerate(pairs)]
    for copy in copies:
        copy.start()
    for copy in copies:
        copy.wait()


def spread_kernel(rows, out):
    for owner in range(out.shape[0]):
        out[owner] = rows[...]


def mix_own_kernel(
    info, own_hbm, neighbours_hbm, weights_hbm, head_hbm, scale_hbm, gain_hbm, bias_hbm, target_hbm,
    own, weights, head, scale, gain, bias, target,
    neighbours, taken, mixed_out, base_out, sems,
):
    load(
        [(own_hbm, own), (neighbours_hbm, neighbours), (weights_hbm, weights), (head_hbm, head),
         (scale_hbm, scale), (gain_hbm, gain), (bias_hbm, bias), (target_hbm, target)],
        sems,
    )
    source = own[...]
    places = relative_places(info, neighbours)
    base_out[...] = mul(head[...], source, NT)
    mixed = weights[CENTRE : CENTRE + 1, :] * source.astype(F32)
    for tap in range(weights.shape[0]):
        if tap != CENTRE:
            rows = tap_rows(places, source, tap)
            taken[tap - (tap > CENTRE)] = rows.astype(BF16)
            mixed = mixed + weights[tap : tap + 1, :] * rows
    mixed_out[...] = mixed


def mix(where, tile, weights, taken_in, mixed_in, taken, mixed_out):
    source = tile[...]
    mixed = mixed_in[...]
    for tap in range(weights.shape[0]):
        if tap != CENTRE:
            rows = tap_rows(where, source, tap)
            slot = tap - (tap > CENTRE)
            taken[slot] = taken_in[slot] + rows.astype(BF16)
            mixed = mixed + weights[tap : tap + 1, :] * rows
    mixed_out[...] = mixed


def mix_pair_kernel(info, tile, neighbours, weights, taken_in, mixed_in, taken, mixed_out):
    mix(pair_places(info, neighbours), tile, weights, taken_in, mixed_in, taken, mixed_out)


def mix_side_kernel(
    info, tile, neighbours, weights, gain, taken_in, mixed_in, taken, mixed_out, normed_out
):
    mix(side_places(info, neighbours), tile, weights, taken_in, mixed_in, taken, mixed_out)
    mixed = mixed_out[...]
    centred = mixed - row_mean(mixed)
    inverse = lax.rsqrt(row_mean(centred * centred) + 1e-06)
    normed_out[...] = (centred * inverse * gain[...]).astype(BF16)


def forward_kernel(
    info, normed, mine, other, bias, base, head, scale,
    act_out, slope_out, forecast_out, up, down, reach,
):
    owners = mine.shape[0]
    half = mine.shape[1] // 2
    for owner in range(owners):
        for side in range(2):
            rows = slice((2 * owner + side) * half, (2 * owner + side + 1) * half)
            up[rows, :] = jnp.where(info[2] == side, mine[owner, :half], other[owner, :half])
            down[rows, :] = jnp.where(info[2] == side, mine[owner, half:], other[owner, half:])
    high, low = halves(head[...].astype(F32) * scale[...])
    product = mul(jnp.concatenate([high, low], axis=0), down[...], NT)
    high, low = halves(product[:8] + product[8:])
    reach[...] = jnp.concatenate([high, low], axis=0)
    forward(normed, up, reach, bias, base, act_out, slope_out, forecast_out)


def forward(normed, up, reach, bias, base, act_out, slope_out, forecast_out):
    rows = normed[...]
    total = base[...]
    for low_edge in range(0, up.shape[0], 256):
        piece = slice(low_edge, low_edge + 256)
        pre = mul(rows, up[piece, :], NT) + bias[:, piece]
        phi = 0.5 + 0.5 * lax.erf(pre * 0.7071067811865476)
        act = (pre * phi).astype(BF16)
        act_out[:, piece] = act
        slope_out[:, piece] = phi + pre * jnp.exp(-0.5 * pre * pre) * 0.3989422804014327
        part = mul(reach[:, piece], act, NT)
        total = total + part[:8] + part[8:]
    forecast_out[...] = total


def backward_kernel(
    mine, other, target, reach, slope, up, mixed, gain, mixed_grad, pre_out, grad_out, loss_out
):
    apart = mine[...] - target[...]
    spread = mine[...] - other[...]
    apart_abs, spread_abs = soft_abs(apart), soft_abs(spread)
    grad = (0.5 * (apart / apart_abs) - 0.5 * (spread / spread_abs)).astype(BF16)
    grad_out[...] = grad
    loss_out[...] = jnp.full(loss_out.shape, jnp.sum(0.5 * apart_abs - 0.25 * spread_abs), F32)
    twice = turned(jnp.concatenate([grad, grad], axis=0))
    normed_grad = jnp.zeros(mixed.shape, F32)
    for low_edge in range(0, up.shape[0], 256):
        piece = slice(low_edge, low_edge + 256)
        pre = (mul(twice, reach[:, piece]) * slope[:, piece]).astype(BF16)
        pre_out[:, piece] = pre
        normed_grad = normed_grad + mul(pre, up[piece, :])
    values = mixed[...]
    centred = values - row_mean(values)
    inverse = lax.rsqrt(row_mean(centred * centred) + 1e-06)
    z = centred * inverse
    gained = normed_grad * gain[...]
    mixed_grad[...] = (
        inverse * (gained - row_mean(gained) - z * row_mean(gained * z))
    ).astype(BF16)


def weights_kernel(
    info, pre_grad, normed, act, grad, features, down, scale, taken, mixed_grad, loss,
    keep, send, small,
):
    normed_t = turned(normed[...])
    summed = mul(grad[...], act[...])
    high, low = halves(summed)
    through = mul(jnp.concatenate([high, low], axis=0), down[...])
    head_part = mul(grad[...], features[...]) + scale[...] * (through[:8] + through[8:])
    flow = mixed_grad[...].astype(F32)
    depth = [
        jnp.sum(taken[k].astype(F32) * flow, axis=0, keepdims=True)
        for k in range(taken.shape[0])
    ]
    depth.insert(CENTRE, jnp.sum(features[...].astype(F32) * flow, axis=0, keepdims=True))
    small[...] = jnp.concatenate([head_part] + depth + [loss[...]], axis=0)
    first = info[2] == 0
    for block in range(keep.shape[0]):
        lanes = slice(block * LANES, (block + 1) * LANES)
        up_part = mul(normed_t, pre_grad[:, lanes])
        lower, higher = up_part[:LANES], up_part[LANES:]
        keep[block, :LANES, :] = jnp.where(first, lower, higher).astype(BF16)
        send[block, :, :] = jnp.where(first, higher, lower).astype(BF16)
        extra = [small[:, :LANES], small[:, LANES:], summed[:, lanes], jnp.zeros((4, LANES), F32)]
        keep[block, LANES:, :] = jnp.concatenate(extra, axis=0).astype(BF16)


def back_kernel(
    info, mine, other, target, reach, slope, up, mixed, gain, normed, act, features, down, scale, taken,
    mixed_grad, grad, keep, send, pre_grad, loss, small,
):
    backward_kernel(
        mine, other, target, reach, slope, up, mixed, gain, mixed_grad, pre_grad, grad, loss
    )
    weights_kernel(
        info, pre_grad, normed, act, grad, features, down, scale, taken, mixed_grad, loss,
        keep, send, small,
    )


def join_kernel(keep, came, joined):
    for block in range(keep.shape[0]):
        main = keep[block, :LANES, :].astype(F32) + came[block].astype(F32)
        joined[block, :LANES, :] = main.astype(BF16)
        joined[block, LANES:, :] = keep[block, LANES:, :]


def sum_kernel(parts, total):
    value = parts[0].astype(F32)
    for part in range(1, parts.shape[0]):
        value = value + parts[part].astype(F32)
    total[...] = value


def final_kernel(factors, info, ours, theirs, head, scale, mean, up, down, depth, head_out):
    loss_factor, factor = factors
    mine, other = ours[:LANES, :], theirs[:LANES, :]
    up[:, :LANES] = jnp.where(info[2] == 0, mine, other).T * factor
    up[:, LANES:] = jnp.where(info[2] == 0, other, mine).T * factor
    extra = ours[LANES:, :] + theirs[LANES:, :]
    small = jnp.concatenate([extra[:18], extra[18:36]], axis=1)
    head_out[...] = small[:8] * factor
    depth[...] = small[8:17] * factor
    mean[0] = jnp.sum(small[17:18, :1]) * loss_factor
    high, low = halves(extra[36:44])
    turn = jnp.concatenate([high, low], axis=0).astype(F32).T.astype(BF16)
    down[...] = mul(turn, jnp.concatenate([head[...], head[...]], axis=0)) * (scale[...] * factor)


def back_taps(total, source, places, weights):
    last = weights.shape[0] - 1
    for tap in range(last + 1):
        if tap != CENTRE:
            total = total + weights[last - tap : last - tap + 1, :] * tap_rows(places, source, tap)
    return total


def input_own_kernel(info, own, neighbours, weights, grad, head, out):
    source = own[...]
    centre = weights.shape[0] - 1 - CENTRE
    total = mul(turned(grad[...]), head[...])
    total = total + weights[centre : centre + 1, :] * source.astype(F32)
    out[...] = back_taps(total, source, relative_places(info, neighbours), weights)


def input_pair_kernel(info, tile, neighbours, weights, partial, out):
    out[...] = back_taps(partial[...], tile[...], pair_places(info, neighbours), weights)


def input_side_kernel(info, tile, neighbours, weights, partial, out):
    total = back_taps(partial[...], tile[...], side_places(info, neighbours), weights)
    out[...] = total.astype(BF16)


def call(
    kernel, outs, scalars, *operands, hbm=0, scratch=(), aliases=None, flops=2000000000, mib=8, smem_outs=(), last=False
):
    smem = pl.BlockSpec(memory_space=pltpu.SMEM)
    out_spec = pl.BlockSpec() if last else pl.BlockSpec(memory_space=pltpu.VMEM)
    kinds = [smem] * scalars + [pl.BlockSpec(memory_space=pltpu.HBM)] * hbm
    kinds = kinds + [pl.BlockSpec()] * (len(operands) - len(kinds))
    return pl.pallas_call(
        kernel,
        out_shape=tuple(jax.ShapeDtypeStruct(shape, dtype) for shape, dtype in outs),
        in_specs=kinds,
        out_specs=tuple(smem if k in smem_outs else out_spec for k in range(len(outs))),
        scratch_shapes=list(scratch),
        input_output_aliases=aliases or {},
        compiler_params=pltpu.CompilerParams(vmem_limit_bytes=mib * 2**20),
        cost_estimate=pl.CostEstimate(flops=flops, bytes_accessed=0, transcendentals=0),
    )(*operands)


def pair_tiles(array):
    count = lax.axis_size("pix")
    inner = [(i, i ^ 1) for i in range(count)]
    outer = [(i, i + 1) for i in range(1, count - 1, 2)]
    outer = outer + [(j, i) for i, j in outer]
    return lax.ppermute(array, "pix", inner), lax.ppermute(array, "pix", outer)


def swap(array):
    return lax.ppermute(array, "mem", [(0, 1), (1, 0)])


def local(
    features,
    neighbours,
    analysis_fields,
    depth_weight,
    norm_gain,
    up_weight,
    up_bias,
    down_weight,
    layer_scale,
    head_matrix,
):
    pixels, channels = features.shape[1:]
    count = lax.axis_size("pix")
    owned_rows = up_weight.shape[0]
    hidden = owned_rows * count
    taps = neighbours.shape[0]
    position, member = lax.axis_index("pix"), lax.axis_index("mem")
    info = jnp.stack([position * pixels, position % 2, member]).astype(jnp.int32)
    own = features[0]
    gain, scale, bias = norm_gain[None], layer_scale[None], up_bias[None]
    by_blocks = owned_rows == LANES
    exact = lax.Precision.HIGHEST
    tile, many = (pixels, channels), (taps - 1, pixels, channels)

    def everywhere(array):
        return lax.all_to_all(array, "pix", split_axis=0, concat_axis=0)

    pair, side = pair_tiles(own)
    if by_blocks:
        half = owned_rows // 2
        rows = jnp.stack([up_weight, down_weight])
        rows = lax.dynamic_slice_in_dim(rows, member * half, half, 1)
        (rows,) = call(
            spread_kernel,
            [((count, owned_rows, channels), BF16)],
            0,
            rows.reshape(owned_rows, channels),
            flops=OWN,
        )
        mine = everywhere(rows)
    else:
        up = lax.all_gather(up_weight, "pix", axis=0, tiled=True)
        down = lax.all_gather(down_weight, "pix", axis=0, tiled=True)
        reach = lax.dot_general(
            head_matrix.astype(F32) * layer_scale, down.astype(F32), NT, precision=exact
        )
        reach = jnp.concatenate(halves(reach), axis=0)
    own, weights, head, scale, gain, bias, target, places, taken, mixed, base = call(
        mix_own_kernel,
        [(tile, BF16), (depth_weight.shape, F32), (head_matrix.shape, BF16),
         ((1, channels), F32), ((1, channels), F32), ((1, hidden), F32), ((8, pixels), F32),
         (neighbours.shape, jnp.int32), (many, BF16), (tile, F32), ((8, pixels), F32)],
        1,
        info, own, neighbours, depth_weight, head_matrix, scale, gain, bias, analysis_fields,
        hbm=8,
        scratch=[pltpu.SemaphoreType.DMA((8,))],
        flops=OWN,
    )
    taken, mixed = call(
        mix_pair_kernel,
        [(many, BF16), (tile, F32)],
        1,
        info, pair, places, weights, taken, mixed,
        aliases={4: 0, 5: 1},
        flops=NEAR,
    )
    taken, mixed, normed = call(
        mix_side_kernel,
        [(many, BF16), (tile, F32), (tile, BF16)],
        1,
        info, side, places, weights, gain, taken, mixed,
        aliases={5: 0, 6: 1},
        flops=NEAR,
    )
    outs = [((pixels, hidden), BF16), ((pixels, hidden), F32), ((8, pixels), F32)]
    if by_blocks:
        mine, normed = lax.optimization_barrier((mine, normed))
        other = swap(mine)
        whole = ((hidden, channels), BF16)
        act, slope, forecast, up, down, reach = call(
            forward_kernel,
            outs + [whole, whole, ((16, hidden), BF16)],
            1,
            info, normed, mine, other, bias, base, head, scale,
        )
    else:
        act, slope, forecast = call(forward, outs, 0, normed, up, reach, bias, base)
    blocks = hidden // LANES
    full = ((blocks, LANES + EXTRA, LANES), BF16)
    mixed_grad, grad, keep, send = call(
        back_kernel,
        [(tile, BF16), ((8, pixels), BF16), full, ((blocks, LANES, LANES), BF16)],
        1,
        info, forecast, swap(forecast), target, reach, slope, up, mixed, gain,
        normed, act, own, down, scale, taken,
        scratch=[pltpu.VMEM((pixels, hidden), BF16), pltpu.VMEM((1, channels), F32),
                 pltpu.VMEM((18, channels), F32)],
        flops=NEAR,
    )
    came = swap(send)
    grad_pair, grad_side = pair_tiles(mixed_grad)
    (joined,) = call(join_kernel, [full], 0, keep, came)
    source, joined = lax.optimization_barrier((mixed_grad, joined))
    (partial,) = call(
        input_own_kernel, [(tile, F32)], 1, info, source, places, weights, grad, head, flops=OWN
    )
    (partial,) = call(
        input_pair_kernel,
        [(tile, F32)],
        1,
        info, grad_pair, places, weights, partial,
        flops=NEAR,
    )
    (input_grad,) = call(
        input_side_kernel,
        [(tile, BF16)],
        1,
        info, grad_side, places, weights, partial,
        flops=NEAR,
        last=True,
    )
    grad_scale = 1.0 / math.sqrt(pixels * count * 2)
    loss_scale = 1.0 / (pixels * count * 8)
    if by_blocks:
        parts, input_grad = lax.optimization_barrier((everywhere(joined), input_grad))
        (total,) = call(sum_kernel, [((LANES + EXTRA, LANES), F32)], 0, parts)
        mean_crps, up_grad, down_grad, depth_grad, head_grad = call(
            functools.partial(final_kernel, (loss_scale, grad_scale)),
            [((1,), F32), ((LANES, channels), F32), ((LANES, channels), F32),
             ((taps, channels), F32), ((8, channels), F32)],
            1,
            info, total, swap(total), head, scale,
            smem_outs=(0,),
            last=True,
        )
        return mean_crps, input_grad[None], up_grad, down_grad, depth_grad, head_grad

    main = joined[:, :LANES].astype(F32)
    main = jnp.stack([main, swap(main)])
    main = jnp.where(member == 0, main, main[::-1])
    rows = jnp.transpose(main, (1, 3, 0, 2)).reshape(hidden, channels)
    up_grad = lax.psum_scatter(rows, "pix", scatter_dimension=0, tiled=True)
    summed = keep[:, LANES + 36 : LANES + 44].astype(F32)
    summed = jnp.transpose(summed + swap(summed), (0, 2, 1)).reshape(hidden, 8)
    summed = lax.psum_scatter(summed, "pix", scatter_dimension=0, tiled=True)
    down_grad = layer_scale * jnp.dot(summed, head_matrix.astype(F32), precision=exact)
    small = keep[0, LANES : LANES + 36].astype(F32).reshape(2, 18, LANES)
    small = jnp.transpose(small, (1, 0, 2)).reshape(18, channels)
    small = lax.psum(small, ("pix", "mem"))
    return (
        small[17, :1] * loss_scale,
        input_grad[None],
        up_grad * grad_scale,
        down_grad * grad_scale,
        small[8:17] * grad_scale,
        small[:8] * grad_scale,
    )


def solution(mesh):
    return jax.shard_map(
        local,
        mesh=mesh,
        in_specs=(
            P("mem", ("groups", "pix"), None),
            P(None, "pix"),
            P(None, ("groups", "pix")),
            P(),
            P(),
            P("pix", None),
            P(),
            P("pix", None),
            P(),
            P(),
        ),
        out_specs=(
            P("groups"),
            P("mem", ("groups", "pix"), None),
            P(("groups", "pix"), None),
            P(("groups", "pix"), None),
            P("groups", None),
            P("groups", None),
        ),
        check_vma=False,
    )
```

```python
import functools
import math

import jax
import jax.numpy as jnp
from jax import lax
from jax.experimental import pallas as pl
from jax.experimental.pallas import tpu as pltpu
from jax.sharding import PartitionSpec as P

F32 = jnp.float32
BF16 = jnp.bfloat16
LANES = 128
EXTRA = 48
CENTRE = 4
NN = (((1,), (0,)), ((), ()))
NT = (((1,), (1,)), ((), ()))
TN = (((0,), (0,)), ((), ()))
FAR = -1e6
NEAR = 50 * 10**9
OWN = 8 * 10**9


def mul(a, b, dims=NN):
    return lax.dot_general(a, b, dims, preferred_element_type=F32)


def halves(values):
    high = values.astype(BF16)
    return high, (values - high.astype(F32)).astype(BF16)


def row_mean(values):
    return jnp.mean(values, axis=-1, keepdims=True)


def soft_abs(values):
    return jnp.sqrt(values * values + 0.04)


def turned(values):
    return values.astype(F32).T.astype(BF16)


def relative_places(info, neighbours):
    table = neighbours[...]
    relative = jnp.where(table >= 0, (table - info[0]).astype(F32), FAR)
    fill = jnp.full((16 - table.shape[0], table.shape[1]), FAR, F32)
    return jnp.concatenate([relative, fill], axis=0).T


def pair_places(info, neighbours):
    pixels = neighbours.shape[1]
    return relative_places(info, neighbours) + jnp.where(info[1] == 0, -pixels, pixels).astype(F32)


def side_places(info, neighbours):
    pixels = neighbours.shape[1]
    return relative_places(info, neighbours) + jnp.where(info[1] == 0, pixels, -pixels).astype(F32)


def tap_rows(places, source, tap):
    shape = (places.shape[0], 256)
    column = lax.broadcasted_iota(jnp.int32, shape, 1).astype(F32).astype(BF16)
    one, zero = jnp.ones((), BF16), jnp.zeros((), BF16)
    chosen = []
    for low_edge in range(0, source.shape[0], 256):
        place = jnp.broadcast_to(places[:, tap : tap + 1] - float(low_edge), shape).astype(BF16)
        chosen.append(jnp.where(column == place, one, zero))
    return mul(jnp.concatenate(chosen, axis=1), source)


def load(pairs, sems):
    copies = [pltpu.make_async_copy(src, dst, sems.at[k]) for k, (src, dst) in enumerate(pairs)]
    for copy in copies:
        copy.start()
    for copy in copies:
        copy.wait()


def spread_kernel(rows, out):
    for owner in range(out.shape[0]):
        out[owner] = rows[...]


def mix_own_kernel(
    info, own_hbm, neighbours_hbm, weights_hbm, head_hbm, scale_hbm, gain_hbm, bias_hbm, target_hbm,
    own, weights, head, scale, gain, bias, target,
    neighbours, taken, mixed_out, base_out, sems,
):
    load(
        [(own_hbm, own), (neighbours_hbm, neighbours), (weights_hbm, weights), (head_hbm, head),
         (scale_hbm, scale), (gain_hbm, gain), (bias_hbm, bias), (target_hbm, target)],
        sems,
    )
    source = own[...]
    places = relative_places(info, neighbours)
    base_out[...] = mul(head[...], source, NT)
    mixed = weights[CENTRE : CENTRE + 1, :] * source.astype(F32)
    for tap in range(weights.shape[0]):
        if tap != CENTRE:
            rows = tap_rows(places, source, tap)
            taken[tap - (tap > CENTRE)] = rows.astype(BF16)
            mixed = mixed + weights[tap : tap + 1, :] * rows
    mixed_out[...] = mixed


def mix(where, tile, weights, taken_in, mixed_in, taken, mixed_out):
    source = tile[...]
    mixed = mixed_in[...]
    for tap in range(weights.shape[0]):
        if tap != CENTRE:
            rows = tap_rows(where, source, tap)
            slot = tap - (tap > CENTRE)
            taken[slot] = taken_in[slot] + rows.astype(BF16)
            mixed = mixed + weights[tap : tap + 1, :] * rows
    mixed_out[...] = mixed


def mix_pair_kernel(info, tile, neighbours, weights, taken_in, mixed_in, taken, mixed_out):
    mix(pair_places(info, neighbours), tile, weights, taken_in, mixed_in, taken, mixed_out)


def mix_side_kernel(
    info, tile, neighbours, weights, gain, taken_in, mixed_in, taken, mixed_out, normed_out
):
    mix(side_places(info, neighbours), tile, weights, taken_in, mixed_in, taken, mixed_out)
    mixed = mixed_out[...]
    centred = mixed - row_mean(mixed)
    inverse = lax.rsqrt(row_mean(centred * centred) + 1e-06)
    normed_out[...] = (centred * inverse * gain[...]).astype(BF16)


def forward_kernel(
    info, normed, mine, other, bias, base, head, scale,
    act_out, slope_out, forecast_out, normed_t, up, down, reach,
):
    owners = mine.shape[0]
    half = mine.shape[1] // 2
    for owner in range(owners):
        for side in range(2):
            rows = slice((2 * owner + side) * half, (2 * owner + side + 1) * half)
            up[rows, :] = jnp.where(info[2] == side, mine[owner, :half], other[owner, :half])
            down[rows, :] = jnp.where(info[2] == side, mine[owner, half:], other[owner, half:])
    high, low = halves(head[...].astype(F32) * scale[...])
    product = mul(jnp.concatenate([high, low], axis=0), down[...], NT)
    high, low = halves(product[:8] + product[8:])
    reach[...] = jnp.concatenate([high, low], axis=0)
    forward(normed, up, reach, bias, base, act_out, slope_out, forecast_out, normed_t)


def forward(normed, up, reach, bias, base, act_out, slope_out, forecast_out, normed_t):
    rows = normed[...]
    normed_t[...] = turned(rows)
    total = base[...]
    for low_edge in range(0, up.shape[0], 256):
        piece = slice(low_edge, low_edge + 256)
        pre = mul(rows, up[piece, :], NT) + bias[:, piece]
        phi = 0.5 + 0.5 * lax.erf(pre * 0.7071067811865476)
        act = (pre * phi).astype(BF16)
        act_out[:, piece] = act
        slope_out[:, piece] = phi + pre * jnp.exp(-0.5 * pre * pre) * 0.3989422804014327
        part = mul(reach[:, piece], act, NT)
        total = total + part[:8] + part[8:]
    forecast_out[...] = total


def backward_kernel(
    mine, other, target, reach, slope, up, mixed, gain, mixed_grad, pre_out, grad_out, loss_out
):
    apart = mine[...] - target[...]
    spread = mine[...] - other[...]
    apart_abs, spread_abs = soft_abs(apart), soft_abs(spread)
    grad = (0.5 * (apart / apart_abs) - 0.5 * (spread / spread_abs)).astype(BF16)
    grad_out[...] = grad
    loss_out[...] = jnp.full(loss_out.shape, jnp.sum(0.5 * apart_abs - 0.25 * spread_abs), F32)
    twice = turned(jnp.concatenate([grad, grad], axis=0))
    normed_grad = jnp.zeros(mixed.shape, F32)
    for low_edge in range(0, up.shape[0], 256):
        piece = slice(low_edge, low_edge + 256)
        pre = (mul(twice, reach[:, piece]) * slope[:, piece]).astype(BF16)
        pre_out[:, piece] = pre
        normed_grad = normed_grad + mul(pre, up[piece, :])
    values = mixed[...]
    centred = values - row_mean(values)
    inverse = lax.rsqrt(row_mean(centred * centred) + 1e-06)
    z = centred * inverse
    gained = normed_grad * gain[...]
    mixed_grad[...] = (
        inverse * (gained - row_mean(gained) - z * row_mean(gained * z))
    ).astype(BF16)


def back_kernel(
    info, mine, other, target, reach, slope, up, mixed, gain, normed_t,
    mixed_grad, grad, send, pre_grad, loss, kept,
):
    backward_kernel(
        mine, other, target, reach, slope, up, mixed, gain, mixed_grad, pre_grad, grad, loss
    )
    first = info[2] == 0
    lower, higher = normed_t[:LANES, :], normed_t[LANES:, :]
    kept[...] = jnp.where(first, lower, higher)
    rows = jnp.where(first, higher, lower)
    for block in range(send.shape[0]):
        lanes = slice(block * LANES, (block + 1) * LANES)
        send[block] = mul(rows, pre_grad[:, lanes]).astype(BF16)


def weights_kernel(
    pre_grad, kept, act, grad, features, down, scale, taken, mixed_grad, loss, came, joined
):
    rows = kept[...]
    summed = mul(grad[...], act[...])
    high, low = halves(summed)
    through = mul(jnp.concatenate([high, low], axis=0), down[...])
    head_part = mul(grad[...], features[...]) + scale[...] * (through[:8] + through[8:])
    flow = mixed_grad[...].astype(F32)
    depth = [
        jnp.sum(taken[k].astype(F32) * flow, axis=0, keepdims=True)
        for k in range(taken.shape[0])
    ]
    depth.insert(CENTRE, jnp.sum(features[...].astype(F32) * flow, axis=0, keepdims=True))
    small = jnp.concatenate([head_part] + depth + [loss[...]], axis=0)
    for block in range(joined.shape[0]):
        lanes = slice(block * LANES, (block + 1) * LANES)
        main = mul(rows, pre_grad[:, lanes]) + came[block].astype(F32)
        joined[block, :LANES, :] = main.astype(BF16)
        extra = [small[:, :LANES], small[:, LANES:], summed[:, lanes], jnp.zeros((4, LANES), F32)]
        joined[block, LANES:, :] = jnp.concatenate(extra, axis=0).astype(BF16)


def sum_kernel(parts, total):
    value = parts[0].astype(F32)
    for part in range(1, parts.shape[0]):
        value = value + parts[part].astype(F32)
    total[...] = value


def final_kernel(factors, info, ours, theirs, head, scale, mean, up, down, depth, head_out):
    loss_factor, factor = factors
    mine, other = ours[:LANES, :], theirs[:LANES, :]
    up[:, :LANES] = jnp.where(info[2] == 0, mine, other).T * factor
    up[:, LANES:] = jnp.where(info[2] == 0, other, mine).T * factor
    extra = ours[LANES:, :] + theirs[LANES:, :]
    small = jnp.concatenate([extra[:18], extra[18:36]], axis=1)
    head_out[...] = small[:8] * factor
    depth[...] = small[8:17] * factor
    mean[0] = jnp.sum(small[17:18, :1]) * loss_factor
    high, low = halves(extra[36:44])
    turn = jnp.concatenate([high, low], axis=0).astype(F32).T.astype(BF16)
    down[...] = mul(turn, jnp.concatenate([head[...], head[...]], axis=0)) * (scale[...] * factor)


def back_taps(total, source, places, weights):
    last = weights.shape[0] - 1
    for tap in range(last + 1):
        if tap != CENTRE:
            total = total + weights[last - tap : last - tap + 1, :] * tap_rows(places, source, tap)
    return total


def input_own_kernel(info, own, neighbours, weights, grad, head, out):
    source = own[...]
    centre = weights.shape[0] - 1 - CENTRE
    total = mul(turned(grad[...]), head[...])
    total = total + weights[centre : centre + 1, :] * source.astype(F32)
    out[...] = back_taps(total, source, relative_places(info, neighbours), weights)


def input_pair_kernel(info, tile, neighbours, weights, partial, out):
    out[...] = back_taps(partial[...], tile[...], pair_places(info, neighbours), weights)


def input_side_kernel(info, tile, neighbours, weights, partial, out):
    total = back_taps(partial[...], tile[...], side_places(info, neighbours), weights)
    out[...] = total.astype(BF16)


def call(
    kernel, outs, scalars, *operands, hbm=0, scratch=(), aliases=None, flops=2000000000, mib=8, smem_outs=(), last=False
):
    smem = pl.BlockSpec(memory_space=pltpu.SMEM)
    out_spec = pl.BlockSpec() if last else pl.BlockSpec(memory_space=pltpu.VMEM)
    kinds = [smem] * scalars + [pl.BlockSpec(memory_space=pltpu.HBM)] * hbm
    kinds = kinds + [pl.BlockSpec()] * (len(operands) - len(kinds))
    return pl.pallas_call(
        kernel,
        out_shape=tuple(jax.ShapeDtypeStruct(shape, dtype) for shape, dtype in outs),
        in_specs=kinds,
        out_specs=tuple(smem if k in smem_outs else out_spec for k in range(len(outs))),
        scratch_shapes=list(scratch),
        input_output_aliases=aliases or {},
        compiler_params=pltpu.CompilerParams(vmem_limit_bytes=mib * 2**20),
        cost_estimate=pl.CostEstimate(flops=flops, bytes_accessed=0, transcendentals=0),
    )(*operands)


def pair_tiles(array):
    count = lax.axis_size("pix")
    inner = [(i, i ^ 1) for i in range(count)]
    outer = [(i, i + 1) for i in range(1, count - 1, 2)]
    outer = outer + [(j, i) for i, j in outer]
    return lax.ppermute(array, "pix", inner), lax.ppermute(array, "pix", outer)


def swap(array):
    return lax.ppermute(array, "mem", [(0, 1), (1, 0)])


def local(
    features,
    neighbours,
    analysis_fields,
    depth_weight,
    norm_gain,
    up_weight,
    up_bias,
    down_weight,
    layer_scale,
    head_matrix,
):
    pixels, channels = features.shape[1:]
    count = lax.axis_size("pix")
    owned_rows = up_weight.shape[0]
    hidden = owned_rows * count
    taps = neighbours.shape[0]
    position, member = lax.axis_index("pix"), lax.axis_index("mem")
    info = jnp.stack([position * pixels, position % 2, member]).astype(jnp.int32)
    own = features[0]
    gain, scale, bias = norm_gain[None], layer_scale[None], up_bias[None]
    by_blocks = owned_rows == LANES
    exact = lax.Precision.HIGHEST
    tile, many = (pixels, channels), (taps - 1, pixels, channels)

    def everywhere(array):
        return lax.all_to_all(array, "pix", split_axis=0, concat_axis=0)

    pair, side = pair_tiles(own)
    if by_blocks:
        half = owned_rows // 2
        rows = jnp.stack([up_weight, down_weight])
        rows = lax.dynamic_slice_in_dim(rows, member * half, half, 1)
        (rows,) = call(
            spread_kernel,
            [((count, owned_rows, channels), BF16)],
            0,
            rows.reshape(owned_rows, channels),
            flops=OWN,
        )
        mine = everywhere(rows)
    else:
        up = lax.all_gather(up_weight, "pix", axis=0, tiled=True)
        down = lax.all_gather(down_weight, "pix", axis=0, tiled=True)
        reach = lax.dot_general(
            head_matrix.astype(F32) * layer_scale, down.astype(F32), NT, precision=exact
        )
        reach = jnp.concatenate(halves(reach), axis=0)
    own, weights, head, scale, gain, bias, target, places, taken, mixed, base = call(
        mix_own_kernel,
        [(tile, BF16), (depth_weight.shape, F32), (head_matrix.shape, BF16),
         ((1, channels), F32), ((1, channels), F32), ((1, hidden), F32), ((8, pixels), F32),
         (neighbours.shape, jnp.int32), (many, BF16), (tile, F32), ((8, pixels), F32)],
        1,
        info, own, neighbours, depth_weight, head_matrix, scale, gain, bias, analysis_fields,
        hbm=8,
        scratch=[pltpu.SemaphoreType.DMA((8,))],
        flops=OWN,
    )
    taken, mixed = call(
        mix_pair_kernel,
        [(many, BF16), (tile, F32)],
        1,
        info, pair, places, weights, taken, mixed,
        aliases={4: 0, 5: 1},
        flops=NEAR,
    )
    taken, mixed, normed = call(
        mix_side_kernel,
        [(many, BF16), (tile, F32), (tile, BF16)],
        1,
        info, side, places, weights, gain, taken, mixed,
        aliases={5: 0, 6: 1},
        flops=NEAR,
    )
    outs = [
        ((pixels, hidden), BF16), ((pixels, hidden), F32), ((8, pixels), F32), ((channels, pixels), BF16)
    ]
    if by_blocks:
        mine, normed = lax.optimization_barrier((mine, normed))
        other = swap(mine)
        whole = ((hidden, channels), BF16)
        act, slope, forecast, normed_t, up, down, reach = call(
            forward_kernel,
            outs + [whole, whole, ((16, hidden), BF16)],
            1,
            info, normed, mine, other, bias, base, head, scale,
        )
    else:
        act, slope, forecast, normed_t = call(forward, outs, 0, normed, up, reach, bias, base)
    blocks = hidden // LANES
    full = ((blocks, LANES + EXTRA, LANES), BF16)
    mixed_grad, grad, send, pre_grad, loss, kept = call(
        back_kernel,
        [(tile, BF16), ((8, pixels), BF16), ((blocks, LANES, LANES), BF16),
         ((pixels, hidden), BF16), ((1, channels), F32), ((LANES, pixels), BF16)],
        1,
        info, forecast, swap(forecast), target, reach, slope, up, mixed, gain, normed_t,
    )
    came = swap(send)
    grad_pair, grad_side = pair_tiles(mixed_grad)
    (joined,) = call(
        weights_kernel,
        [full],
        0,
        pre_grad, kept, act, grad, own, down, scale, taken, mixed_grad, loss, came,
    )
    source, joined = lax.optimization_barrier((mixed_grad, joined))
    (partial,) = call(
        input_own_kernel, [(tile, F32)], 1, info, source, places, weights, grad, head, flops=OWN
    )
    (partial,) = call(
        input_pair_kernel,
        [(tile, F32)],
        1,
        info, grad_pair, places, weights, partial,
        flops=NEAR,
    )
    (input_grad,) = call(
        input_side_kernel,
        [(tile, BF16)],
        1,
        info, grad_side, places, weights, partial,
        flops=NEAR,
        last=True,
    )
    grad_scale = 1.0 / math.sqrt(pixels * count * 2)
    loss_scale = 1.0 / (pixels * count * 8)
    if by_blocks:
        parts, input_grad = lax.optimization_barrier((everywhere(joined), input_grad))
        (total,) = call(sum_kernel, [((LANES + EXTRA, LANES), F32)], 0, parts)
        mean_crps, up_grad, down_grad, depth_grad, head_grad = call(
            functools.partial(final_kernel, (loss_scale, grad_scale)),
            [((1,), F32), ((LANES, channels), F32), ((LANES, channels), F32),
             ((taps, channels), F32), ((8, channels), F32)],
            1,
            info, total, swap(total), head, scale,
            smem_outs=(0,),
            last=True,
        )
        return mean_crps, input_grad[None], up_grad, down_grad, depth_grad, head_grad

    main = joined[:, :LANES].astype(F32)
    main = jnp.stack([main, swap(main)])
    main = jnp.where(member == 0, main, main[::-1])
    rows = jnp.transpose(main, (1, 3, 0, 2)).reshape(hidden, channels)
    up_grad = lax.psum_scatter(rows, "pix", scatter_dimension=0, tiled=True)
    summed = joined[:, LANES + 36 : LANES + 44].astype(F32)
    summed = jnp.transpose(summed + swap(summed), (0, 2, 1)).reshape(hidden, 8)
    summed = lax.psum_scatter(summed, "pix", scatter_dimension=0, tiled=True)
    down_grad = layer_scale * jnp.dot(summed, head_matrix.astype(F32), precision=exact)
    small = joined[0, LANES : LANES + 36].astype(F32).reshape(2, 18, LANES)
    small = jnp.transpose(small, (1, 0, 2)).reshape(18, channels)
    small = lax.psum(small, ("pix", "mem"))
    return (
        small[17, :1] * loss_scale,
        input_grad[None],
        up_grad * grad_scale,
        down_grad * grad_scale,
        small[8:17] * grad_scale,
        small[:8] * grad_scale,
    )


def solution(mesh):
    return jax.shard_map(
        local,
        mesh=mesh,
        in_specs=(
            P("mem", ("groups", "pix"), None),
            P(None, "pix"),
            P(None, ("groups", "pix")),
            P(),
            P(),
            P("pix", None),
            P(),
            P("pix", None),
            P(),
            P(),
        ),
        out_specs=(
            P("groups"),
            P("mem", ("groups", "pix"), None),
            P(("groups", "pix"), None),
            P(("groups", "pix"), None),
            P("groups", None),
            P("groups", None),
        ),
        check_vma=False,
    )
```

```python
import functools
import math

import jax
import jax.numpy as jnp
from jax import lax
from jax.experimental import pallas as pl
from jax.experimental.pallas import tpu as pltpu
from jax.sharding import PartitionSpec as P

F32 = jnp.float32
BF16 = jnp.bfloat16
LANES = 128
EXTRA = 48
CENTRE = 4
NN = (((1,), (0,)), ((), ()))
NT = (((1,), (1,)), ((), ()))
TN = (((0,), (0,)), ((), ()))
FAR = -1e6
NEAR = 50 * 10**9
OWN = 8 * 10**9


def mul(a, b, dims=NN):
    return lax.dot_general(a, b, dims, preferred_element_type=F32)


def halves(values):
    high = values.astype(BF16)
    return high, (values - high.astype(F32)).astype(BF16)


def row_mean(values):
    return jnp.mean(values, axis=-1, keepdims=True)


def soft_abs(values):
    return jnp.sqrt(values * values + 0.04)


def turned(values):
    return values.astype(F32).T.astype(BF16)


def relative_places(info, neighbours):
    table = neighbours[...]
    relative = jnp.where(table >= 0, (table - info[0]).astype(F32), FAR)
    fill = jnp.full((16 - table.shape[0], table.shape[1]), FAR, F32)
    return jnp.concatenate([relative, fill], axis=0).T


def pair_places(info, neighbours):
    pixels = neighbours.shape[1]
    return relative_places(info, neighbours) + jnp.where(info[1] == 0, -pixels, pixels).astype(F32)


def side_places(info, neighbours):
    pixels = neighbours.shape[1]
    return relative_places(info, neighbours) + jnp.where(info[1] == 0, pixels, -pixels).astype(F32)


def tap_rows(places, source, tap):
    shape = (places.shape[0], 256)
    column = lax.broadcasted_iota(jnp.int32, shape, 1).astype(F32).astype(BF16)
    one, zero = jnp.ones((), BF16), jnp.zeros((), BF16)
    chosen = []
    for low_edge in range(0, source.shape[0], 256):
        place = jnp.broadcast_to(places[:, tap : tap + 1] - float(low_edge), shape).astype(BF16)
        chosen.append(jnp.where(column == place, one, zero))
    return mul(jnp.concatenate(chosen, axis=1), source)


def load(pairs, sems):
    copies = [pltpu.make_async_copy(src, dst, sems.at[k]) for k, (src, dst) in enumerate(pairs)]
    for copy in copies:
        copy.start()
    for copy in copies:
        copy.wait()


def spread_kernel(rows, out):
    for owner in range(out.shape[0]):
        out[owner] = rows[...]


def by_owner(split, first, mine, other):
    if not split:
        return mine + other
    blocks = []
    for a, b in zip(mine, other):
        low, high = jnp.where(first, a, b), jnp.where(first, b, a)
        left = lax.broadcasted_iota(jnp.int32, a.shape, 1) < LANES // 2
        blocks.append(jnp.where(left, low, pltpu.roll(high, LANES // 2, 1)))
        blocks.append(jnp.where(left, pltpu.roll(low, LANES // 2, 1), high))
    return blocks


def by_half(split, first, blocks):
    if not split:
        middle = len(blocks) // 2
        return blocks[:middle], blocks[middle:]
    mine, other = [], []
    for a, b in zip(blocks[::2], blocks[1::2]):
        left = lax.broadcasted_iota(jnp.int32, a.shape, 1) < LANES // 2
        low = jnp.where(left, a, pltpu.roll(b, LANES // 2, 1))
        high = jnp.where(left, pltpu.roll(a, LANES // 2, 1), b)
        mine.append(jnp.where(first, low, high))
        other.append(jnp.where(first, high, low))
    return mine, other


def lane_blocks(ref):
    return [ref[:, low : low + LANES] for low in range(0, ref.shape[1], LANES)]


def mix_own_kernel(
    split, info, own_hbm, neighbours_hbm, weights_hbm, head_hbm, scale_hbm, gain_hbm, bias_hbm, target_hbm,
    own, weights, head, scale, gain, bias, target,
    neighbours, taken, mixed_out, base_out, bias_mine, bias_other, sems,
):
    load(
        [(own_hbm, own), (neighbours_hbm, neighbours), (weights_hbm, weights), (head_hbm, head),
         (scale_hbm, scale), (gain_hbm, gain), (bias_hbm, bias), (target_hbm, target)],
        sems,
    )
    whole = [jnp.broadcast_to(block, (8, LANES)) for block in lane_blocks(bias)]
    mine, other = by_half(split, info[2] == 0, whole)
    bias_mine[...] = jnp.concatenate(mine, axis=1)
    bias_other[...] = jnp.concatenate(other, axis=1)
    source = own[...]
    places = relative_places(info, neighbours)
    base_out[...] = mul(head[...], source, NT)
    mixed = weights[CENTRE : CENTRE + 1, :] * source.astype(F32)
    for tap in range(weights.shape[0]):
        if tap != CENTRE:
            rows = tap_rows(places, source, tap)
            taken[tap - (tap > CENTRE)] = rows.astype(BF16)
            mixed = mixed + weights[tap : tap + 1, :] * rows
    mixed_out[...] = mixed


def mix(where, tile, weights, taken_in, mixed_in, taken, mixed_out):
    source = tile[...]
    mixed = mixed_in[...]
    for tap in range(weights.shape[0]):
        if tap != CENTRE:
            rows = tap_rows(where, source, tap)
            slot = tap - (tap > CENTRE)
            taken[slot] = taken_in[slot] + rows.astype(BF16)
            mixed = mixed + weights[tap : tap + 1, :] * rows
    mixed_out[...] = mixed


def mix_pair_kernel(info, tile, neighbours, weights, taken_in, mixed_in, taken, mixed_out):
    mix(pair_places(info, neighbours), tile, weights, taken_in, mixed_in, taken, mixed_out)


def mix_side_kernel(
    info, tile, neighbours, weights, gain, taken_in, mixed_in, taken, mixed_out, normed_out
):
    mix(side_places(info, neighbours), tile, weights, taken_in, mixed_in, taken, mixed_out)
    mixed = mixed_out[...]
    centred = mixed - row_mean(mixed)
    inverse = lax.rsqrt(row_mean(centred * centred) + 1e-06)
    normed_out[...] = (centred * inverse * gain[...]).astype(BF16)


def forward_kernel(
    normed, part, bias, base, head, scale, act_out, slope_out, forecast_out, up, down, reach
):
    owners, half = part.shape[0], part.shape[1] // 2
    for owner in range(owners):
        rows = slice(owner * half, (owner + 1) * half)
        up[rows, :] = part[owner, :half]
        down[rows, :] = part[owner, half:]
    high, low = halves(head[...].astype(F32) * scale[...])
    product = mul(jnp.concatenate([high, low], axis=0), down[...], NT)
    high, low = halves(product[:8] + product[8:])
    reach[...] = jnp.concatenate([high, low], axis=0)
    rows = normed[...]
    total = base[...]
    for low_edge in range(0, up.shape[0], 256):
        piece = slice(low_edge, low_edge + 256)
        pre = mul(rows, up[piece, :], NT) + bias[:1, piece]
        phi = 0.5 + 0.5 * lax.erf(pre * 0.7071067811865476)
        act = (pre * phi).astype(BF16)
        act_out[:, piece] = act
        slope_out[:, piece] = phi + pre * jnp.exp(-0.5 * pre * pre) * 0.3989422804014327
        product = mul(reach[:, piece], act, NT)
        total = total + product[:8] + product[8:]
    forecast_out[...] = total


def first_kernel(
    normed, part, bias, base, head, scale,
    act_out, slope_out, forecast_out, up, down, reach, normed_t,
):
    normed_t[...] = turned(normed[...])
    forward_kernel(
        normed, part, bias, base, head, scale, act_out, slope_out, forecast_out, up, down, reach
    )


def backward_kernel(
    mine, other, target, reaches, slopes, ups, mixed, gain, mixed_grad, pre_outs, grad_out, loss_out
):
    apart = mine[...] - target[...]
    spread = mine[...] - other[...]
    apart_abs, spread_abs = soft_abs(apart), soft_abs(spread)
    grad = (0.5 * (apart / apart_abs) - 0.5 * (spread / spread_abs)).astype(BF16)
    grad_out[...] = grad
    loss_out[...] = jnp.full(loss_out.shape, jnp.sum(0.5 * apart_abs - 0.25 * spread_abs), F32)
    twice = turned(jnp.concatenate([grad, grad], axis=0))
    normed_grad = jnp.zeros(mixed.shape, F32)
    for reach, slope, up, pre_out in zip(reaches, slopes, ups, pre_outs):
        for low_edge in range(0, up.shape[0], 256):
            piece = slice(low_edge, low_edge + 256)
            pre = (mul(twice, reach[:, piece]) * slope[:, piece]).astype(BF16)
            pre_out[:, piece] = pre
            normed_grad = normed_grad + mul(pre, up[piece, :])
    values = mixed[...]
    centred = values - row_mean(values)
    inverse = lax.rsqrt(row_mean(centred * centred) + 1e-06)
    z = centred * inverse
    gained = normed_grad * gain[...]
    mixed_grad[...] = (
        inverse * (gained - row_mean(gained) - z * row_mean(gained * z))
    ).astype(BF16)


def up_blocks(split, first, rows, pre_grads):
    products = [[mul(rows, block) for block in lane_blocks(pre)] for pre in pre_grads]
    return by_owner(split, first, *products)


def back_kernel(
    split, info, mine, other, target, reach_a, reach_b, slope_a, slope_b, up_a, up_b, mixed, gain, normed_t,
    mixed_grad, grad, send, pre_a, pre_b, loss, kept,
):
    backward_kernel(
        mine, other, target, (reach_a, reach_b), (slope_a, slope_b), (up_a, up_b), mixed, gain,
        mixed_grad, (pre_a, pre_b), grad, loss,
    )
    first = info[2] == 0
    lower, higher = normed_t[:LANES, :], normed_t[LANES:, :]
    kept[...] = jnp.where(first, lower, higher)
    rows = jnp.where(first, higher, lower)
    for block, value in enumerate(up_blocks(split, first, rows, (pre_a, pre_b))):
        send[block] = value.astype(BF16)


def weights_kernel(
    split, info, pre_a, pre_b, kept, act_a, act_b, grad, features, down_a, down_b, scale, taken, mixed_grad,
    loss, came, joined
):
    first = info[2] == 0
    sums, through = [], 0.0
    for act, down in ((act_a, down_a), (act_b, down_b)):
        summed = mul(grad[...], act[...])
        high, low = halves(summed)
        product = mul(jnp.concatenate([high, low], axis=0), down[...])
        through = through + product[:8] + product[8:]
        sums.append(lane_blocks(summed))
    sums = by_owner(split, first, *sums)
    head_part = mul(grad[...], features[...]) + scale[...] * through
    flow = mixed_grad[...].astype(F32)
    depth = [
        jnp.sum(taken[k].astype(F32) * flow, axis=0, keepdims=True)
        for k in range(taken.shape[0])
    ]
    depth.insert(CENTRE, jnp.sum(features[...].astype(F32) * flow, axis=0, keepdims=True))
    rest = jnp.concatenate(depth + [loss[...]], axis=0)
    small = jnp.concatenate(
        [head_part[:, :LANES], head_part[:, LANES:], rest[:, :LANES], rest[:, LANES:],
         jnp.zeros((4, LANES), F32)],
        axis=0,
    )
    for block, value in enumerate(up_blocks(split, first, kept[...], (pre_a, pre_b))):
        joined[block, :LANES, :] = (value + came[block].astype(F32)).astype(BF16)
        extra = jnp.concatenate([sums[block], small], axis=0)
        joined[block, LANES:, :] = extra.astype(BF16)


def sum_kernel(parts, total):
    value = parts[0].astype(F32)
    for part in range(1, parts.shape[0]):
        value = value + parts[part].astype(F32)
    total[...] = value


def final_kernel(factors, info, ours, theirs, head, scale, mean, up, down, depth, head_out):
    loss_factor, factor = factors
    mine, other = ours[:LANES, :], theirs[:LANES, :]
    up[:, :LANES] = jnp.where(info[2] == 0, mine, other).T * factor
    up[:, LANES:] = jnp.where(info[2] == 0, other, mine).T * factor
    extra = ours[LANES:, :] + theirs[LANES:, :]
    head_out[:, :LANES] = extra[8:16] * factor
    head_out[:, LANES:] = extra[16:24] * factor
    depth[:, :LANES] = extra[24:33] * factor
    depth[:, LANES:] = extra[34:43] * factor
    mean[0] = jnp.sum(extra[33:34, :1]) * loss_factor
    high, low = halves(extra[:8])
    turn = jnp.concatenate([high, low], axis=0).astype(F32).T.astype(BF16)
    down[...] = mul(turn, jnp.concatenate([head[...], head[...]], axis=0)) * (scale[...] * factor)


def back_taps(total, source, places, weights):
    last = weights.shape[0] - 1
    for tap in range(last + 1):
        if tap != CENTRE:
            total = total + weights[last - tap : last - tap + 1, :] * tap_rows(places, source, tap)
    return total


def input_own_kernel(info, own, neighbours, weights, grad, head, out):
    source = own[...]
    centre = weights.shape[0] - 1 - CENTRE
    total = mul(turned(grad[...]), head[...])
    total = total + weights[centre : centre + 1, :] * source.astype(F32)
    out[...] = back_taps(total, source, relative_places(info, neighbours), weights)


def input_pair_kernel(info, tile, neighbours, weights, partial, out):
    out[...] = back_taps(partial[...], tile[...], pair_places(info, neighbours), weights)


def input_side_kernel(info, tile, neighbours, weights, partial, out):
    total = back_taps(partial[...], tile[...], side_places(info, neighbours), weights)
    out[...] = total.astype(BF16)


def call(
    kernel, outs, scalars, *operands, hbm=0, scratch=(), aliases=None, flops=2000000000, mib=8, smem_outs=(), last=False
):
    smem = pl.BlockSpec(memory_space=pltpu.SMEM)
    out_spec = pl.BlockSpec() if last else pl.BlockSpec(memory_space=pltpu.VMEM)
    kinds = [smem] * scalars + [pl.BlockSpec(memory_space=pltpu.HBM)] * hbm
    kinds = kinds + [pl.BlockSpec()] * (len(operands) - len(kinds))
    return pl.pallas_call(
        kernel,
        out_shape=tuple(jax.ShapeDtypeStruct(shape, dtype) for shape, dtype in outs),
        in_specs=kinds,
        out_specs=tuple(smem if k in smem_outs else out_spec for k in range(len(outs))),
        scratch_shapes=list(scratch),
        input_output_aliases=aliases or {},
        compiler_params=pltpu.CompilerParams(vmem_limit_bytes=mib * 2**20),
        cost_estimate=pl.CostEstimate(flops=flops, bytes_accessed=0, transcendentals=0),
    )(*operands)


def pair_tiles(array):
    count = lax.axis_size("pix")
    inner = [(i, i ^ 1) for i in range(count)]
    outer = [(i, i + 1) for i in range(1, count - 1, 2)]
    outer = outer + [(j, i) for i, j in outer]
    return lax.ppermute(array, "pix", inner), lax.ppermute(array, "pix", outer)


def swap(array):
    return lax.ppermute(array, "mem", [(0, 1), (1, 0)])


def local(
    features,
    neighbours,
    analysis_fields,
    depth_weight,
    norm_gain,
    up_weight,
    up_bias,
    down_weight,
    layer_scale,
    head_matrix,
):
    pixels, channels = features.shape[1:]
    count = lax.axis_size("pix")
    owned_rows = up_weight.shape[0]
    hidden = owned_rows * count
    taps = neighbours.shape[0]
    position, member = lax.axis_index("pix"), lax.axis_index("mem")
    info = jnp.stack([position * pixels, position % 2, member]).astype(jnp.int32)
    own = features[0]
    gain, scale, bias = norm_gain[None], layer_scale[None], up_bias[None]
    by_blocks = owned_rows == LANES
    exact = lax.Precision.HIGHEST
    tile, many = (pixels, channels), (taps - 1, pixels, channels)

    def everywhere(array):
        return lax.all_to_all(array, "pix", split_axis=0, concat_axis=0)

    pair, side = pair_tiles(own)
    if by_blocks:
        half = owned_rows // 2
        rows = jnp.stack([up_weight, down_weight])
        rows = lax.dynamic_slice_in_dim(rows, member * half, half, 1)
        (rows,) = call(
            spread_kernel,
            [((count, owned_rows, channels), BF16)],
            0,
            rows.reshape(owned_rows, channels),
            flops=OWN,
        )
        mine = everywhere(rows)
    else:
        up = lax.all_gather(up_weight, "pix", axis=0, tiled=True)
        down = lax.all_gather(down_weight, "pix", axis=0, tiled=True)
        part = (8, hidden // 16, channels)
        mine, other = [
            jnp.concatenate([up[rows].reshape(part), down[rows].reshape(part)], axis=1)
            for rows in (slice(0, hidden // 2), slice(hidden // 2, hidden))
        ]
    short = ((8, hidden // 2), F32)
    own, weights, head, scale, gain, _, target, places, taken, mixed, base, bias_mine, bias_other = call(
        functools.partial(mix_own_kernel, by_blocks),
        [(tile, BF16), (depth_weight.shape, F32), (head_matrix.shape, BF16),
         ((1, channels), F32), ((1, channels), F32), ((1, hidden), F32), ((8, pixels), F32),
         (neighbours.shape, jnp.int32), (many, BF16), (tile, F32), ((8, pixels), F32), short, short],
        1,
        info, own, neighbours, depth_weight, head_matrix, scale, gain, bias, analysis_fields,
        hbm=8,
        scratch=[pltpu.SemaphoreType.DMA((8,))],
        flops=OWN,
    )
    taken, mixed = call(
        mix_pair_kernel,
        [(many, BF16), (tile, F32)],
        1,
        info, pair, places, weights, taken, mixed,
        aliases={4: 0, 5: 1},
        flops=NEAR,
    )
    taken, mixed, normed = call(
        mix_side_kernel,
        [(many, BF16), (tile, F32), (tile, BF16)],
        1,
        info, side, places, weights, gain, taken, mixed,
        aliases={5: 0, 6: 1},
        flops=NEAR,
    )
    if by_blocks:
        mine, normed = lax.optimization_barrier((mine, normed))
        other = swap(mine)
    whole = ((hidden // 2, channels), BF16)
    outs = [
        ((pixels, hidden // 2), BF16), ((pixels, hidden // 2), F32), ((8, pixels), F32),
        whole, whole, ((16, hidden // 2), BF16),
    ]
    act_a, slope_a, base, up_a, down_a, reach_a, normed_t = call(
        first_kernel,
        outs + [((channels, pixels), BF16)],
        0,
        normed, mine, bias_mine, base, head, scale,
    )
    act_b, slope_b, forecast, up_b, down_b, reach_b = call(
        forward_kernel, outs, 0, normed, other, bias_other, base, head, scale
    )
    blocks = hidden // LANES
    full = ((blocks, LANES + EXTRA, LANES), BF16)
    pre = ((pixels, hidden // 2), BF16)
    mixed_grad, grad, send, pre_a, pre_b, loss, kept = call(
        functools.partial(back_kernel, by_blocks),
        [(tile, BF16), ((8, pixels), BF16), ((blocks, LANES, LANES), BF16),
         pre, pre, ((1, channels), F32), ((LANES, pixels), BF16)],
        1,
        info, forecast, swap(forecast), target, reach_a, reach_b, slope_a, slope_b, up_a, up_b,
        mixed, gain, normed_t,
    )
    came = swap(send)
    grad_pair, grad_side = pair_tiles(mixed_grad)
    (joined,) = call(
        functools.partial(weights_kernel, by_blocks),
        [full],
        1,
        info, pre_a, pre_b, kept, act_a, act_b, grad, own, down_a, down_b, scale, taken, mixed_grad, loss, came,
    )
    source, joined = lax.optimization_barrier((mixed_grad, joined))
    (partial,) = call(
        input_own_kernel, [(tile, F32)], 1, info, source, places, weights, grad, head, flops=OWN
    )
    (partial,) = call(
        input_pair_kernel,
        [(tile, F32)],
        1,
        info, grad_pair, places, weights, partial,
        flops=NEAR,
    )
    (input_grad,) = call(
        input_side_kernel,
        [(tile, BF16)],
        1,
        info, grad_side, places, weights, partial,
        flops=NEAR,
        last=True,
    )
    grad_scale = 1.0 / math.sqrt(pixels * count * 2)
    loss_scale = 1.0 / (pixels * count * 8)
    if by_blocks:
        parts, input_grad = lax.optimization_barrier((everywhere(joined), input_grad))
        (total,) = call(sum_kernel, [((LANES + EXTRA, LANES), F32)], 0, parts)
        mean_crps, up_grad, down_grad, depth_grad, head_grad = call(
            functools.partial(final_kernel, (loss_scale, grad_scale)),
            [((1,), F32), ((LANES, channels), F32), ((LANES, channels), F32),
             ((taps, channels), F32), ((8, channels), F32)],
            1,
            info, total, swap(total), head, scale,
            smem_outs=(0,),
            last=True,
        )
        return mean_crps, input_grad[None], up_grad, down_grad, depth_grad, head_grad

    main = joined[:, :LANES].astype(F32)
    main = jnp.stack([main, swap(main)])
    main = jnp.where(member == 0, main, main[::-1])
    rows = jnp.transpose(main, (1, 3, 0, 2)).reshape(hidden, channels)
    up_grad = lax.psum_scatter(rows, "pix", scatter_dimension=0, tiled=True)
    summed = joined[:, LANES : LANES + 8].astype(F32)
    summed = jnp.transpose(summed + swap(summed), (0, 2, 1)).reshape(hidden, 8)
    summed = lax.psum_scatter(summed, "pix", scatter_dimension=0, tiled=True)
    down_grad = layer_scale * jnp.dot(summed, head_matrix.astype(F32), precision=exact)
    small = joined[0, LANES + 8 : LANES + 44].astype(F32)
    head_rows = jnp.concatenate([small[:8], small[8:16]], axis=1)
    rest = jnp.concatenate([small[16:26], small[26:36]], axis=1)
    head_rows, rest = lax.psum((head_rows, rest), ("pix", "mem"))
    return (
        rest[9, :1] * loss_scale,
        input_grad[None],
        up_grad * grad_scale,
        down_grad * grad_scale,
        rest[:9] * grad_scale,
        head_rows * grad_scale,
    )


def solution(mesh):
    return jax.shard_map(
        local,
        mesh=mesh,
        in_specs=(
            P("mem", ("groups", "pix"), None),
            P(None, "pix"),
            P(None, ("groups", "pix")),
            P(),
            P(),
            P("pix", None),
            P(),
            P("pix", None),
            P(),
            P(),
        ),
        out_specs=(
            P("groups"),
            P("mem", ("groups", "pix"), None),
            P(("groups", "pix"), None),
            P(("groups", "pix"), None),
            P("groups", None),
            P("groups", None),
        ),
        check_vma=False,
    )
```

```python
import functools
import math

import jax
import jax.numpy as jnp
from jax import lax
from jax.experimental import pallas as pl
from jax.experimental.pallas import tpu as pltpu
from jax.sharding import PartitionSpec as P

F32 = jnp.float32
BF16 = jnp.bfloat16
LANES = 128
EXTRA = 48
CENTRE = 4
NN = (((1,), (0,)), ((), ()))
NT = (((1,), (1,)), ((), ()))
TN = (((0,), (0,)), ((), ()))
FAR = -1e6
NEAR = 50 * 10**9
OWN = 8 * 10**9


def mul(a, b, dims=NN):
    return lax.dot_general(a, b, dims, preferred_element_type=F32)


def halves(values):
    high = values.astype(BF16)
    return high, (values - high.astype(F32)).astype(BF16)


def row_mean(values):
    return jnp.mean(values, axis=-1, keepdims=True)


def soft_abs(values):
    return jnp.sqrt(values * values + 0.04)


def turned(values):
    return values.astype(F32).T.astype(BF16)


def relative_places(info, neighbours):
    table = neighbours[...]
    relative = jnp.where(table >= 0, (table - info[0]).astype(F32), FAR)
    fill = jnp.full((16 - table.shape[0], table.shape[1]), FAR, F32)
    return jnp.concatenate([relative, fill], axis=0).T


def pair_places(info, neighbours):
    pixels = neighbours.shape[1]
    return relative_places(info, neighbours) + jnp.where(info[1] == 0, -pixels, pixels).astype(F32)


def side_places(info, neighbours):
    pixels = neighbours.shape[1]
    return relative_places(info, neighbours) + jnp.where(info[1] == 0, pixels, -pixels).astype(F32)


def outer_places(info, neighbours):
    relative = relative_places(info, neighbours)
    pixels = float(neighbours.shape[1])
    after, before = relative >= pixels, relative < 0
    even = jnp.where(after, relative - pixels, jnp.where(before, relative + 2 * pixels, FAR))
    odd = jnp.where(before, relative + pixels, jnp.where(after, relative, FAR))
    return jnp.where(info[1] == 0, even, odd)


def tap_rows(places, source, tap):
    shape = (places.shape[0], 256)
    column = lax.broadcasted_iota(jnp.int32, shape, 1).astype(F32).astype(BF16)
    one, zero = jnp.ones((), BF16), jnp.zeros((), BF16)
    chosen = []
    for low_edge in range(0, source.shape[0], 256):
        place = jnp.broadcast_to(places[:, tap : tap + 1] - float(low_edge), shape).astype(BF16)
        chosen.append(jnp.where(column == place, one, zero))
    return mul(jnp.concatenate(chosen, axis=1), source)


def load(pairs, sems):
    copies = [pltpu.make_async_copy(src, dst, sems.at[k]) for k, (src, dst) in enumerate(pairs)]
    for copy in copies:
        copy.start()
    for copy in copies:
        copy.wait()


def spread_kernel(rows, out):
    for owner in range(out.shape[0]):
        out[owner] = rows[...]


def by_owner(split, first, mine, other):
    if not split:
        return mine + other
    blocks = []
    for a, b in zip(mine, other):
        low, high = jnp.where(first, a, b), jnp.where(first, b, a)
        left = lax.broadcasted_iota(jnp.int32, a.shape, 1) < LANES // 2
        blocks.append(jnp.where(left, low, pltpu.roll(high, LANES // 2, 1)))
        blocks.append(jnp.where(left, pltpu.roll(low, LANES // 2, 1), high))
    return blocks


def by_half(split, first, blocks):
    if not split:
        middle = len(blocks) // 2
        return blocks[:middle], blocks[middle:]
    mine, other = [], []
    for a, b in zip(blocks[::2], blocks[1::2]):
        left = lax.broadcasted_iota(jnp.int32, a.shape, 1) < LANES // 2
        low = jnp.where(left, a, pltpu.roll(b, LANES // 2, 1))
        high = jnp.where(left, pltpu.roll(a, LANES // 2, 1), b)
        mine.append(jnp.where(first, low, high))
        other.append(jnp.where(first, high, low))
    return mine, other


def lane_blocks(ref):
    return [ref[:, low : low + LANES] for low in range(0, ref.shape[1], LANES)]


def mix_own_kernel(
    split, info, own_hbm, neighbours_hbm, weights_hbm, scale_hbm, gain_hbm, bias_hbm, target_hbm, head_in,
    own, weights, head, scale, gain, bias, target,
    neighbours, taken, mixed_out, base_out, bias_mine, bias_other, sems,
):
    load(
        [(own_hbm, own), (neighbours_hbm, neighbours), (weights_hbm, weights), (scale_hbm, scale),
         (gain_hbm, gain), (bias_hbm, bias), (target_hbm, target)],
        sems,
    )
    head[...] = head_in[...]
    whole = [jnp.broadcast_to(block, (8, LANES)) for block in lane_blocks(bias)]
    mine, other = by_half(split, info[2] == 0, whole)
    bias_mine[...] = jnp.concatenate(mine, axis=1)
    bias_other[...] = jnp.concatenate(other, axis=1)
    source = own[...]
    places = relative_places(info, neighbours)
    base_out[...] = mul(head[...], source, NT)
    mixed = weights[CENTRE : CENTRE + 1, :] * source.astype(F32)
    for tap in range(weights.shape[0]):
        if tap != CENTRE:
            rows = tap_rows(places, source, tap)
            taken[tap - (tap > CENTRE)] = rows.astype(BF16)
            mixed = mixed + weights[tap : tap + 1, :] * rows
    mixed_out[...] = mixed


def mix(where, tile, weights, taken_in, mixed_in, taken, mixed_out):
    source = tile[...]
    mixed = mixed_in[...]
    for tap in range(weights.shape[0]):
        if tap != CENTRE:
            rows = tap_rows(where, source, tap)
            slot = tap - (tap > CENTRE)
            taken[slot] = taken_in[slot] + rows.astype(BF16)
            mixed = mixed + weights[tap : tap + 1, :] * rows
    mixed_out[...] = mixed


def mix_pair_kernel(info, tile, neighbours, weights, taken_in, mixed_in, taken, mixed_out):
    mix(pair_places(info, neighbours), tile, weights, taken_in, mixed_in, taken, mixed_out)


def mix_side_kernel(
    info, tile, neighbours, weights, gain, taken_in, mixed_in, taken, mixed_out, normed_out
):
    mix(side_places(info, neighbours), tile, weights, taken_in, mixed_in, taken, mixed_out)
    mixed = mixed_out[...]
    centred = mixed - row_mean(mixed)
    inverse = lax.rsqrt(row_mean(centred * centred) + 1e-06)
    normed_out[...] = (centred * inverse * gain[...]).astype(BF16)


def forward_kernel(
    normed, part, bias, base, head, scale, act_out, slope_out, forecast_out, up, down, reach
):
    owners, half = part.shape[0], part.shape[1] // 2
    for owner in range(owners):
        rows = slice(owner * half, (owner + 1) * half)
        up[rows, :] = part[owner, :half]
        down[rows, :] = part[owner, half:]
    high, low = halves(head[...].astype(F32) * scale[...])
    product = mul(jnp.concatenate([high, low], axis=0), down[...], NT)
    high, low = halves(product[:8] + product[8:])
    reach[...] = jnp.concatenate([high, low], axis=0)
    rows = normed[...]
    total = base[...]
    for low_edge in range(0, up.shape[0], 256):
        piece = slice(low_edge, low_edge + 256)
        pre = mul(rows, up[piece, :], NT) + bias[:1, piece]
        phi = 0.5 + 0.5 * lax.erf(pre * 0.7071067811865476)
        act = (pre * phi).astype(BF16)
        act_out[:, piece] = act
        slope_out[:, piece] = phi + pre * jnp.exp(-0.5 * pre * pre) * 0.3989422804014327
        product = mul(reach[:, piece], act, NT)
        total = total + product[:8] + product[8:]
    forecast_out[...] = total


def first_kernel(
    normed, part, bias, base, head, scale,
    act_out, slope_out, forecast_out, up, down, reach, normed_t,
):
    normed_t[...] = turned(normed[...])
    forward_kernel(
        normed, part, bias, base, head, scale, act_out, slope_out, forecast_out, up, down, reach
    )


def backward_kernel(
    mine, other, target, reaches, slopes, ups, mixed, gain, mixed_grad, pre_outs, grad_out, loss_out
):
    apart = mine[...] - target[...]
    spread = mine[...] - other[...]
    apart_abs, spread_abs = soft_abs(apart), soft_abs(spread)
    grad = (0.5 * (apart / apart_abs) - 0.5 * (spread / spread_abs)).astype(BF16)
    grad_out[...] = grad
    loss_out[...] = jnp.full(loss_out.shape, jnp.sum(0.5 * apart_abs - 0.25 * spread_abs), F32)
    twice = turned(jnp.concatenate([grad, grad], axis=0))
    normed_grad = jnp.zeros(mixed.shape, F32)
    for reach, slope, up, pre_out in zip(reaches, slopes, ups, pre_outs):
        for low_edge in range(0, up.shape[0], 256):
            piece = slice(low_edge, low_edge + 256)
            pre = (mul(twice, reach[:, piece]) * slope[:, piece]).astype(BF16)
            pre_out[:, piece] = pre
            normed_grad = normed_grad + mul(pre, up[piece, :])
    values = mixed[...]
    centred = values - row_mean(values)
    inverse = lax.rsqrt(row_mean(centred * centred) + 1e-06)
    z = centred * inverse
    gained = normed_grad * gain[...]
    mixed_grad[...] = (
        inverse * (gained - row_mean(gained) - z * row_mean(gained * z))
    ).astype(BF16)


def up_blocks(split, first, rows, pre_grads):
    products = [[mul(rows, block) for block in lane_blocks(pre)] for pre in pre_grads]
    return by_owner(split, first, *products)


def back_kernel(
    split, info, mine, other, target, reach_a, reach_b, slope_a, slope_b, up_a, up_b, mixed, gain, normed_t,
    mixed_grad, grad, send, pre_a, pre_b, loss, kept,
):
    backward_kernel(
        mine, other, target, (reach_a, reach_b), (slope_a, slope_b), (up_a, up_b), mixed, gain,
        mixed_grad, (pre_a, pre_b), grad, loss,
    )
    first = info[2] == 0
    lower, higher = normed_t[:LANES, :], normed_t[LANES:, :]
    kept[...] = jnp.where(first, lower, higher)
    rows = jnp.where(first, higher, lower)
    for block, value in enumerate(up_blocks(split, first, rows, (pre_a, pre_b))):
        send[block] = value.astype(BF16)


def weights_kernel(
    split, info, pre_a, pre_b, kept, act_a, act_b, grad, features, down_a, down_b, scale, taken, mixed_grad,
    loss, came, joined
):
    first = info[2] == 0
    sums, through = [], 0.0
    for act, down in ((act_a, down_a), (act_b, down_b)):
        summed = mul(grad[...], act[...])
        high, low = halves(summed)
        product = mul(jnp.concatenate([high, low], axis=0), down[...])
        through = through + product[:8] + product[8:]
        sums.append(lane_blocks(summed))
    sums = by_owner(split, first, *sums)
    head_part = mul(grad[...], features[...]) + scale[...] * through
    flow = mixed_grad[...].astype(F32)
    depth = [
        jnp.sum(taken[k].astype(F32) * flow, axis=0, keepdims=True)
        for k in range(taken.shape[0])
    ]
    depth.insert(CENTRE, jnp.sum(features[...].astype(F32) * flow, axis=0, keepdims=True))
    rest = jnp.concatenate(depth + [loss[...]], axis=0)
    small = jnp.concatenate(
        [head_part[:, :LANES], head_part[:, LANES:], rest[:, :LANES], rest[:, LANES:],
         jnp.zeros((4, LANES), F32)],
        axis=0,
    )
    for block, value in enumerate(up_blocks(split, first, kept[...], (pre_a, pre_b))):
        joined[block, :LANES, :] = (value + came[block].astype(F32)).astype(BF16)
        extra = jnp.concatenate([sums[block], small], axis=0)
        joined[block, LANES:, :] = extra.astype(BF16)


def sum_kernel(parts, total):
    value = parts[0].astype(F32)
    for part in range(1, parts.shape[0]):
        value = value + parts[part].astype(F32)
    total[...] = value


def final_kernel(factors, info, ours, theirs, head, scale, mean, up, down, depth, head_out):
    loss_factor, factor = factors
    mine, other = ours[:LANES, :], theirs[:LANES, :]
    up[:, :LANES] = jnp.where(info[2] == 0, mine, other).T * factor
    up[:, LANES:] = jnp.where(info[2] == 0, other, mine).T * factor
    extra = ours[LANES:, :] + theirs[LANES:, :]
    head_out[:, :LANES] = extra[8:16] * factor
    head_out[:, LANES:] = extra[16:24] * factor
    depth[:, :LANES] = extra[24:33] * factor
    depth[:, LANES:] = extra[34:43] * factor
    mean[0] = jnp.sum(extra[33:34, :1]) * loss_factor
    high, low = halves(extra[:8])
    turn = jnp.concatenate([high, low], axis=0).astype(F32).T.astype(BF16)
    down[...] = mul(turn, jnp.concatenate([head[...], head[...]], axis=0)) * (scale[...] * factor)


def back_taps(total, source, places, weights):
    last = weights.shape[0] - 1
    for tap in range(last + 1):
        if tap != CENTRE:
            total = total + weights[last - tap : last - tap + 1, :] * tap_rows(places, source, tap)
    return total


def input_own_kernel(info, own, neighbours, weights, grad, head, out):
    source = own[...]
    centre = weights.shape[0] - 1 - CENTRE
    total = mul(turned(grad[...]), head[...])
    total = total + weights[centre : centre + 1, :] * source.astype(F32)
    out[...] = back_taps(total, source, relative_places(info, neighbours), weights)


def input_outer_kernel(info, side, pair, neighbours, weights, partial, out):
    source = jnp.concatenate([pair[...], side[...]], axis=0)
    total = back_taps(partial[...], source, outer_places(info, neighbours), weights)
    out[...] = total.astype(BF16)


def call(
    kernel, outs, scalars, *operands, hbm=0, scratch=(), aliases=None, flops=2000000000, mib=8, smem_outs=(), last=False
):
    smem = pl.BlockSpec(memory_space=pltpu.SMEM)
    out_spec = pl.BlockSpec() if last else pl.BlockSpec(memory_space=pltpu.VMEM)
    kinds = [smem] * scalars + [pl.BlockSpec(memory_space=pltpu.HBM)] * hbm
    kinds = kinds + [pl.BlockSpec()] * (len(operands) - len(kinds))
    return pl.pallas_call(
        kernel,
        out_shape=tuple(jax.ShapeDtypeStruct(shape, dtype) for shape, dtype in outs),
        in_specs=kinds,
        out_specs=tuple(smem if k in smem_outs else out_spec for k in range(len(outs))),
        scratch_shapes=list(scratch),
        input_output_aliases=aliases or {},
        compiler_params=pltpu.CompilerParams(vmem_limit_bytes=mib * 2**20),
        cost_estimate=pl.CostEstimate(flops=flops, bytes_accessed=0, transcendentals=0),
    )(*operands)


def pair_tiles(array):
    count = lax.axis_size("pix")
    inner = [(i, i ^ 1) for i in range(count)]
    outer = [(i, i + 1) for i in range(1, count - 1, 2)]
    outer = outer + [(j, i) for i, j in outer]
    return lax.ppermute(array, "pix", inner), lax.ppermute(array, "pix", outer)


def swap(array):
    return lax.ppermute(array, "mem", [(0, 1), (1, 0)])


def local(
    features,
    neighbours,
    analysis_fields,
    depth_weight,
    norm_gain,
    up_weight,
    up_bias,
    down_weight,
    layer_scale,
    head_matrix,
):
    pixels, channels = features.shape[1:]
    count = lax.axis_size("pix")
    owned_rows = up_weight.shape[0]
    hidden = owned_rows * count
    taps = neighbours.shape[0]
    position, member = lax.axis_index("pix"), lax.axis_index("mem")
    info = jnp.stack([position * pixels, position % 2, member]).astype(jnp.int32)
    own = features[0]
    gain, scale, bias = norm_gain[None], layer_scale[None], up_bias[None]
    by_blocks = owned_rows == LANES
    exact = lax.Precision.HIGHEST
    tile, many = (pixels, channels), (taps - 1, pixels, channels)

    def everywhere(array):
        return lax.all_to_all(array, "pix", split_axis=0, concat_axis=0)

    pair, side = pair_tiles(own)
    if by_blocks:
        half = owned_rows // 2
        rows = jnp.stack([up_weight, down_weight])
        rows = lax.dynamic_slice_in_dim(rows, member * half, half, 1)
        (rows,) = call(
            spread_kernel,
            [((count, owned_rows, channels), BF16)],
            0,
            rows.reshape(owned_rows, channels),
            flops=OWN,
        )
        mine = everywhere(rows)
    else:
        up = lax.all_gather(up_weight, "pix", axis=0, tiled=True)
        down = lax.all_gather(down_weight, "pix", axis=0, tiled=True)
        part = (8, hidden // 16, channels)
        mine, other = [
            jnp.concatenate([up[rows].reshape(part), down[rows].reshape(part)], axis=1)
            for rows in (slice(0, hidden // 2), slice(hidden // 2, hidden))
        ]
    short = ((8, hidden // 2), F32)
    own, weights, head, scale, gain, _, target, places, taken, mixed, base, bias_mine, bias_other = call(
        functools.partial(mix_own_kernel, by_blocks),
        [(tile, BF16), (depth_weight.shape, F32), (head_matrix.shape, BF16),
         ((1, channels), F32), ((1, channels), F32), ((1, hidden), F32), ((8, pixels), F32),
         (neighbours.shape, jnp.int32), (many, BF16), (tile, F32), ((8, pixels), F32), short, short],
        1,
        info, own, neighbours, depth_weight, scale, gain, bias, analysis_fields, head_matrix,
        hbm=7,
        scratch=[pltpu.SemaphoreType.DMA((7,))],
        flops=OWN,
    )
    taken, mixed = call(
        mix_pair_kernel,
        [(many, BF16), (tile, F32)],
        1,
        info, pair, places, weights, taken, mixed,
        aliases={4: 0, 5: 1},
        flops=NEAR,
    )
    taken, mixed, normed = call(
        mix_side_kernel,
        [(many, BF16), (tile, F32), (tile, BF16)],
        1,
        info, side, places, weights, gain, taken, mixed,
        aliases={5: 0, 6: 1},
        flops=NEAR,
    )
    if by_blocks:
        mine, normed = lax.optimization_barrier((mine, normed))
        other = swap(mine)
    whole = ((hidden // 2, channels), BF16)
    outs = [
        ((pixels, hidden // 2), BF16), ((pixels, hidden // 2), F32), ((8, pixels), F32),
        whole, whole, ((16, hidden // 2), BF16),
    ]
    act_a, slope_a, base, up_a, down_a, reach_a, normed_t = call(
        first_kernel,
        outs + [((channels, pixels), BF16)],
        0,
        normed, mine, bias_mine, base, head, scale,
    )
    act_b, slope_b, forecast, up_b, down_b, reach_b = call(
        forward_kernel, outs, 0, normed, other, bias_other, base, head, scale
    )
    blocks = hidden // LANES
    full = ((blocks, LANES + EXTRA, LANES), BF16)
    pre = ((pixels, hidden // 2), BF16)
    mixed_grad, grad, send, pre_a, pre_b, loss, kept = call(
        functools.partial(back_kernel, by_blocks),
        [(tile, BF16), ((8, pixels), BF16), ((blocks, LANES, LANES), BF16),
         pre, pre, ((1, channels), F32), ((LANES, pixels), BF16)],
        1,
        info, forecast, swap(forecast), target, reach_a, reach_b, slope_a, slope_b, up_a, up_b,
        mixed, gain, normed_t,
    )
    came = swap(send)
    grad_pair, grad_side = pair_tiles(mixed_grad)
    (joined,) = call(
        functools.partial(weights_kernel, by_blocks),
        [full],
        1,
        info, pre_a, pre_b, kept, act_a, act_b, grad, own, down_a, down_b, scale, taken, mixed_grad, loss, came,
    )
    source, joined = lax.optimization_barrier((mixed_grad, joined))
    (partial,) = call(
        input_own_kernel, [(tile, F32)], 1, info, source, places, weights, grad, head, flops=OWN
    )
    (input_grad,) = call(
        input_outer_kernel,
        [(tile, BF16)],
        1,
        info, grad_side, grad_pair, places, weights, partial,
        flops=NEAR,
        last=True,
    )
    grad_scale = 1.0 / math.sqrt(pixels * count * 2)
    loss_scale = 1.0 / (pixels * count * 8)
    if by_blocks:
        parts, input_grad = lax.optimization_barrier((everywhere(joined), input_grad))
        (total,) = call(sum_kernel, [((LANES + EXTRA, LANES), F32)], 0, parts)
        mean_crps, up_grad, down_grad, depth_grad, head_grad = call(
            functools.partial(final_kernel, (loss_scale, grad_scale)),
            [((1,), F32), ((LANES, channels), F32), ((LANES, channels), F32),
             ((taps, channels), F32), ((8, channels), F32)],
            1,
            info, total, swap(total), head, scale,
            smem_outs=(0,),
            last=True,
        )
        return mean_crps, input_grad[None], up_grad, down_grad, depth_grad, head_grad

    main = joined[:, :LANES].astype(F32)
    main = jnp.stack([main, swap(main)])
    main = jnp.where(member == 0, main, main[::-1])
    rows = jnp.transpose(main, (1, 3, 0, 2)).reshape(hidden, channels)
    up_grad = lax.psum_scatter(rows, "pix", scatter_dimension=0, tiled=True)
    summed = joined[:, LANES : LANES + 8].astype(F32)
    summed = jnp.transpose(summed + swap(summed), (0, 2, 1)).reshape(hidden, 8)
    summed = lax.psum_scatter(summed, "pix", scatter_dimension=0, tiled=True)
    down_grad = layer_scale * jnp.dot(summed, head_matrix.astype(F32), precision=exact)
    small = joined[0, LANES + 8 : LANES + 44].astype(F32)
    head_rows = jnp.concatenate([small[:8], small[8:16]], axis=1)
    rest = jnp.concatenate([small[16:26], small[26:36]], axis=1)
    head_rows, rest = lax.psum((head_rows, rest), ("pix", "mem"))
    return (
        rest[9, :1] * loss_scale,
        input_grad[None],
        up_grad * grad_scale,
        down_grad * grad_scale,
        rest[:9] * grad_scale,
        head_rows * grad_scale,
    )


def solution(mesh):
    return jax.shard_map(
        local,
        mesh=mesh,
        in_specs=(
            P("mem", ("groups", "pix"), None),
            P(None, "pix"),
            P(None, ("groups", "pix")),
            P(),
            P(),
            P("pix", None),
            P(),
            P("pix", None),
            P(),
            P(),
        ),
        out_specs=(
            P("groups"),
            P("mem", ("groups", "pix"), None),
            P(("groups", "pix"), None),
            P(("groups", "pix"), None),
            P("groups", None),
            P("groups", None),
        ),
        check_vma=False,
    )
```
